32 devices in a mesh: seq: 8 (over z, y), batch: 4 (over x, core).
Axes of the slice: x: 2, y: 2, z: 4, core: 2. Of those that a mesh axis runs over, the one named last changes fastest.
Arguments:
- queries: bfloat16 [4096, 4096], P(('batch', 'seq')), parts along dimension 0
- keys: bfloat16 [4096, 4096], P(('batch', 'seq')), parts along dimension 0
- values: bfloat16 [4096, 4096], P(('batch', 'seq')), parts along dimension 0, may hold values from -6 to 6
- out_grad: bfloat16 [4096, 4096], P(('batch', 'seq')), parts along dimension 0, may hold values from -6 to 6
- key_blocks: int32 [128, 16, 12], P('batch'), parts along dimension 0, may hold values from -1 to 15, as said below
- dilation: int32 [128], P('batch'), parts along dimension 0, may hold values from 1 to 729, as said below
Outputs:
- attended: bfloat16 [4096, 4096], P(('batch', 'seq')), parts along dimension 0
- queries_grad: bfloat16 [4096, 4096], P(('batch', 'seq')), parts along dimension 0
- keys_grad: bfloat16 [4096, 4096], P(('batch', 'seq')), parts along dimension 0
- values_grad: bfloat16 [4096, 4096], P(('batch', 'seq')), parts along dimension 0
The draws below stay inside these ranges and needn't reach their ends.
There are 4 independent parts, one for each index of `batch`. The reference program is written for one: setup_inputs(seed, part) draws one part's arguments, and reference() takes and returns one part's arrays. A program takes and returns all parts, laid end to end along the dimension named above; each array names one. Nothing has to cross between parts.
Inputs may be any that keep to these rules, and one draw needn't show every extreme that they name: `key_blocks`: in every row the first entry is the query block itself; the listed blocks are distinct, not after the query block, and stand before the -1 entries. Some head lists 12 blocks for each of its last query blocks. `dilation`: every value is a power of three.
All inputs are finite; a program needn't handle non-finite values.
Results may differ from the reference program's by a relative error of at most 0.012.
Values may be sent and summed in bfloat16 or wider, within the bound.
A program may use at most 64 MiB of HBM per device.

```python
import math
import jax
import jax.numpy as jnp
from jax import lax

HEADS = 32
HEAD_DIM = 128
BLOCK = 64
SLOTS = 12
D = 4096
SEQLEN = 1024
QBLOCKS = 16


def drawn_pair(key):
    base = jax.random.fold_in(key, 7)
    first, second = jax.random.split(base, 2)
    query_noise = jnp.clip(jax.random.normal(first, (SEQLEN, HEADS * HEAD_DIM), jnp.float32), -6.0, 6.0)
    key_noise = jnp.clip(jax.random.normal(second, (SEQLEN, HEADS * HEAD_DIM), jnp.float32), -6.0, 6.0)
    return (query_noise, key_noise)


def draw_queries(key, part):
    return drawn_pair(key)[0].astype(jnp.bfloat16)


def draw_keys(key, part):
    return drawn_pair(key)[1].astype(jnp.bfloat16)


def sparse_pattern(key):
    base = jax.random.fold_in(key, 19)
    key_one, key_two, key_three, key_four = jax.random.split(base, 4)
    head_ids = jnp.arange(HEADS, dtype=jnp.int32)
    heavy = jax.random.randint(key_four, (), 0, HEADS, dtype=jnp.int32)
    powers = jnp.array([1, 3, 9, 27, 81, 243, 729], jnp.int32)
    spacing = powers[jax.random.randint(key_one, (HEADS,), 0, 7, dtype=jnp.int32)]
    spacing = jnp.where(head_ids == heavy, 1, jnp.where(head_ids == (heavy + 1) % HEADS, 729, spacing))
    stride = jax.random.randint(key_two, (HEADS,), 1, 3, dtype=jnp.int32)
    stride = jnp.where(head_ids == heavy, 1, stride)
    reaches = jnp.array([2, 3, 4, 6, 8], jnp.int32)
    reach = reaches[jax.random.randint(key_three, (HEADS,), 0, 5, dtype=jnp.int32)]
    reach = jnp.where(head_ids == heavy, SLOTS, reach)
    query_ids = jnp.arange(QBLOCKS, dtype=jnp.int32)[None, :, None]
    slot_ids = jnp.arange(SLOTS, dtype=jnp.int32)[None, None, :]
    listed = query_ids - slot_ids * stride[:, None, None]
    valid = (slot_ids < reach[:, None, None]) & (listed >= 0)
    return (spacing, jnp.where(valid, listed, -1).astype(jnp.int32))


def draw_key_blocks(key, part):
    return sparse_pattern(key)[1]


def draw_dilation(key, part):
    return sparse_pattern(key)[0]


def shard_levels(rng, extent, pieces, low, largest):
    loudness, own = 1.0, jax.random.fold_in(rng, 6)
    for dim, blocks in pieces:
        heights = jnp.exp(jax.random.uniform(jax.random.fold_in(own, dim), (blocks,), jnp.float32, low / len(pieces), largest / len(pieces)))
        loudness = loudness * jnp.repeat(heights, extent[dim] // blocks).reshape([-1 if axis == dim else 1 for axis in range(len(extent))])
    return loudness


def centred(rng, dims, deviation, most, pieces=(), held_as=jnp.bfloat16):
    level = shard_levels(rng, dims, pieces, -0.22, 0.18) if pieces else 1.0
    values = jax.random.normal(rng, dims, jnp.float32) * deviation * level
    return jnp.minimum(jnp.maximum(values, -most), most).astype(held_as)


def setup_inputs(seed: int = 0, part: int = 0) -> dict:
    key_list = jax.random.split(jax.random.key(seed), 7)
    part_splits = jax.random.split(jax.random.fold_in(key_list[6], part), 7)
    return {
        "queries": draw_queries(jax.random.fold_in(jax.random.fold_in(key_list[6], part), 71), part),
        "keys": draw_keys(jax.random.fold_in(jax.random.fold_in(key_list[6], part), 71), part),
        "values": centred(part_splits[2], (SEQLEN, D), 1.0, 6.0, ((0, 8),)),
        "out_grad": centred(part_splits[3], (SEQLEN, D), 1.0, 6.0, ((0, 8),)),
        "key_blocks": draw_key_blocks(jax.random.fold_in(jax.random.fold_in(key_list[6], part), 71), part),
        "dilation": draw_dilation(jax.random.fold_in(jax.random.fold_in(key_list[6], part), 71), part),
    }


very_low = -1e+30

def split_heads(rows):
    return rows.reshape(QBLOCKS, BLOCK, HEADS, HEAD_DIM).transpose(2, 0, 1, 3)

def join_heads(per_head):
    return per_head.transpose(1, 2, 0, 3).reshape(SEQLEN, HEADS * HEAD_DIM)

def one_head(operands):
    head_queries, head_keys, head_values, head_grads, block_rows, spacing = operands
    score_scale = 1.0 / math.sqrt(HEAD_DIM)
    valid = block_rows >= 0
    chosen = jnp.maximum(block_rows, 0).astype(jnp.int32)
    keys_tiles = head_keys[chosen].reshape(QBLOCKS, SLOTS * BLOCK, HEAD_DIM).astype(jnp.float32)
    values_tiles = head_values[chosen].reshape(QBLOCKS, SLOTS * BLOCK, HEAD_DIM).astype(jnp.float32)
    query_ids = jnp.arange(QBLOCKS, dtype=jnp.int32)
    offsets = lax.broadcasted_iota(jnp.int32, (BLOCK, BLOCK), 0) - lax.broadcasted_iota(jnp.int32, (BLOCK, BLOCK), 1)
    distance = ((query_ids[:, None] - chosen) * BLOCK)[:, None, :, None] + offsets[None, :, None, :]
    allowed = valid[:, None, :, None] & (distance >= 0) & (distance % spacing == 0)
    allowed = allowed.reshape(QBLOCKS, BLOCK, SLOTS * BLOCK)
    queries32 = head_queries.astype(jnp.float32)
    grads32 = head_grads.astype(jnp.float32)
    scores = jnp.einsum('gae,gke->gak', queries32, keys_tiles) * score_scale
    scores = jnp.where(allowed, scores, very_low)
    row_top = lax.optimization_barrier(jnp.max(scores, axis=2, keepdims=True))
    expos = jnp.exp(scores - row_top)
    weights = expos / lax.optimization_barrier(jnp.sum(expos, axis=2, keepdims=True))
    weights16 = lax.optimization_barrier(weights.astype(jnp.bfloat16))
    weights_back = weights16.astype(jnp.float32)
    attended = jnp.einsum('gak,gke->gae', weights_back, values_tiles).astype(jnp.bfloat16)
    attended_back = lax.optimization_barrier(attended).astype(jnp.float32)
    delta = lax.optimization_barrier(jnp.sum(grads32 * attended_back, axis=2, keepdims=True))
    dweights = jnp.einsum('gae,gke->gak', grads32, values_tiles)
    dscores16 = lax.optimization_barrier((weights * (dweights - delta)).astype(jnp.bfloat16))
    dscores_back = dscores16.astype(jnp.float32)
    queries_grad = (jnp.einsum('gak,gke->gae', dscores_back, keys_tiles) * score_scale).astype(jnp.bfloat16)
    keys_parts = (jnp.einsum('gak,gae->gke', dscores_back, queries32) * score_scale).reshape(QBLOCKS * SLOTS, BLOCK, HEAD_DIM)
    values_parts = jnp.einsum('gak,gae->gke', weights_back, grads32).reshape(QBLOCKS * SLOTS, BLOCK, HEAD_DIM)
    flat_ids = chosen.reshape(-1)
    keys_grad = jnp.zeros((QBLOCKS, BLOCK, HEAD_DIM), jnp.float32).at[flat_ids].add(keys_parts).astype(jnp.bfloat16)
    values_grad = jnp.zeros((QBLOCKS, BLOCK, HEAD_DIM), jnp.float32).at[flat_ids].add(values_parts).astype(jnp.bfloat16)
    return (attended, queries_grad, keys_grad, values_grad)

def reference(queries, keys, values, out_grad, key_blocks, dilation):
    results = lax.map(one_head, (split_heads(queries), split_heads(keys), split_heads(values), split_heads(out_grad), key_blocks, dilation))
    return (join_heads(results[0]), join_heads(results[1]), join_heads(results[2]), join_heads(results[3]))
```

```python
import functools
import math

import jax
import jax.numpy as jnp
from jax import lax
from jax.experimental import pallas as pl
from jax.experimental.pallas import tpu as pltpu
from jax.sharding import PartitionSpec as P

HEADS = 32
HEAD_DIM = 128
BLOCK = 64

very_low = -1e30
MESH = pl.DeviceIdType.MESH


def dot(a, b, dims):
    return lax.dot_general(a, b, (dims, ((), ())), preferred_element_type=jnp.float32)


LAST = ((1,), (1,))
PLAIN = ((1,), (0,))
FIRST = ((0,), (0,))


def build_masks(head, lists_ref, dilation_ref, row_codes, key_codes):
    blocks, slots = lists_ref.shape[1], lists_ref.shape[2]
    seq = row_codes.shape[1]
    spacing = dilation_ref[head].astype(jnp.float32)
    inverse = 1.0 / jnp.full((1, 128), spacing, jnp.float32)

    def residue(ids, inv):
        ids = ids.astype(jnp.float32)
        return ids - spacing * jnp.floor((ids + 0.5) * inv)

    lists = lists_ref[head]
    key_ids = lax.broadcasted_iota(jnp.int32, (blocks, blocks), 1)
    member = jnp.zeros((blocks, blocks), jnp.float32)
    for slot in range(slots):
        member = jnp.where(lists[:, slot : slot + 1] == key_ids, 1.0, member)
    spread = (
        lax.broadcasted_iota(jnp.int32, (blocks, seq), 1) // BLOCK
        == lax.broadcasted_iota(jnp.int32, (blocks, seq), 0)
    )
    listed = dot(member, spread.astype(jnp.float32), FIRST)
    query_ids = lax.broadcasted_iota(jnp.int32, (blocks, seq), 1)
    row_codes[...] = jnp.where(listed > 0.5, residue(query_ids, inverse[:, :1]), -1.0)
    key_codes[...] = residue(lax.broadcasted_iota(jnp.int32, (seq, 128), 0), inverse)


def attend_tile(start, reach, diagonal_only, tile, chunk, ins, outs, row_codes, key_codes, scratch):
    queries, keys, values, grads = ins
    attended, queries_grad = outs
    keys_t, values_t, keys_sum, values_sum = scratch
    scale = 1.0 / math.sqrt(HEAD_DIM)
    rows = pl.ds(start, tile)
    query, grad = queries[rows, :], grads[rows, :]
    chunks = reach // chunk
    query_ids = start + lax.broadcasted_iota(jnp.int32, (chunk, tile), 1)
    scores = []
    for c in range(chunks):
        span = slice(c * chunk, (c + 1) * chunk)
        raw = dot(keys[span, :], query, LAST)
        codes = key_codes[span, :]
        codes = jnp.concatenate([codes] * (tile // 128), axis=1) if tile > 128 else codes
        first = c * chunk // BLOCK
        wanted = jnp.concatenate(
            [
                jnp.broadcast_to(row_codes[first + b : first + b + 1, rows], (BLOCK, tile))
                for b in range(chunk // BLOCK)
            ],
            axis=0,
        )
        seen = codes == wanted
        if not diagonal_only or c == chunks - 1:
            key_ids = c * chunk + lax.broadcasted_iota(jnp.int32, (chunk, tile), 0)
            seen = seen & (key_ids <= query_ids)
        scores.append(jnp.where(seen, raw, very_low / scale))
    top = functools.reduce(jnp.maximum, [jnp.max(s, axis=0, keepdims=True) for s in scores])
    expos = [jnp.exp2((s - top) * (scale * math.log2(math.e))) for s in scores]
    total = sum(jnp.sum(e, axis=0, keepdims=True) for e in expos)
    share = 1.0 / total
    weights = [e * share for e in expos]
    weights16 = [w.astype(jnp.bfloat16) for w in weights]
    out_t = sum(
        dot(values_t[:, c * chunk : (c + 1) * chunk], weights16[c], PLAIN) for c in range(chunks)
    )
    out16 = jnp.transpose(out_t).astype(jnp.bfloat16)
    attended[rows, :] = out16
    product_t = jnp.transpose(grad.astype(jnp.float32) * out16.astype(jnp.float32))
    delta = jnp.sum(product_t, axis=0, keepdims=True)
    query_t = None
    for c in range(chunks):
        span = slice(c * chunk, (c + 1) * chunk)
        values_sum[span, :] += dot(weights16[c], grad, PLAIN)
        dweights = dot(values[span, :], grad, LAST)
        dscores16 = (weights[c] * (dweights - delta)).astype(jnp.bfloat16)
        keys_sum[span, :] += dot(dscores16, query, PLAIN)
        part = dot(keys_t[:, span], dscores16, PLAIN)
        query_t = part if query_t is None else query_t + part
    queries_grad[rows, :] = jnp.transpose(query_t * scale).astype(jnp.bfloat16)


def attend_head(ins, outs, row_codes, key_codes, scratch):
    keys_t, values_t, keys_sum, values_sum = scratch
    _, keys, values, _ = ins
    attended, queries_grad, keys_grad, values_grad = outs
    seq = keys.shape[0]
    keys_t[...] = jnp.transpose(keys[...].astype(jnp.float32)).astype(jnp.bfloat16)
    values_t[...] = jnp.transpose(values[...].astype(jnp.float32)).astype(jnp.bfloat16)
    keys_sum[...] = jnp.zeros_like(keys_sum)
    values_sum[...] = jnp.zeros_like(values_sum)
    tile_outs = (attended, queries_grad)
    if seq <= 1024:
        for index in range(seq // 256):
            attend_tile(
                index * 256, (index + 1) * 256, True, 256, 256, ins, tile_outs, row_codes, key_codes, scratch
            )
    else:

        def one(index, carry):
            start = pl.multiple_of(index * 128, 128)
            attend_tile(start, seq, False, 128, 256, ins, tile_outs, row_codes, key_codes, scratch)
            return carry

        lax.fori_loop(0, seq // 128, one, 0)
    keys_grad[...] = (keys_sum[...] * (1.0 / math.sqrt(HEAD_DIM))).astype(jnp.bfloat16)
    values_grad[...] = values_sum[...].astype(jnp.bfloat16)


def kernel(
    n,
    heads,
    queries,
    keys,
    values,
    grads,
    lists_ref,
    dilation_ref,
    attended,
    queries_grad,
    keys_grad,
    values_grad,
    held,
    made,
    row_codes,
    key_codes,
    keys_t,
    values_t,
    keys_sum,
    values_sum,
    in_send,
    in_recv,
    out_send,
    out_recv,
):
    me = lax.axis_index("seq")
    tokens = queries.shape[0]
    sources = (queries, keys, values, grads)
    targets = (attended, queries_grad, keys_grad, values_grad)
    my_rows = pl.ds(pl.multiple_of(me * tokens, tokens), tokens)

    def columns(owner, head):
        return pl.ds(pl.multiple_of((owner * heads + head) * HEAD_DIM, HEAD_DIM), HEAD_DIM)

    barrier = pltpu.get_barrier_semaphore()

    def greet(step, carry):
        pl.semaphore_signal(
            barrier, inc=1, device_id={"seq": lax.rem(me + step, n)}, device_id_type=MESH
        )
        return carry

    lax.fori_loop(1, n, greet, 0)
    pl.semaphore_wait(barrier, n - 1)

    def send_head(head, carry):
        def send_one(step, inner):
            other = lax.rem(me + step, n)
            for index, source in enumerate(sources):
                pltpu.make_async_remote_copy(
                    src_ref=source.at[:, columns(other, head)],
                    dst_ref=held.at[head, index, my_rows, :],
                    send_sem=in_send.at[head],
                    recv_sem=in_recv.at[head],
                    device_id={"seq": other},
                    device_id_type=MESH,
                ).start()
            return inner

        for index, source in enumerate(sources):
            pltpu.make_async_copy(
                source.at[:, columns(me, head)], held.at[head, index, my_rows, :], in_recv.at[head]
            ).start()
        lax.fori_loop(1, n, send_one, 0)
        return carry

    lax.fori_loop(0, heads, send_head, 0)

    def work_head(head, carry):
        build_masks(me * heads + head, lists_ref, dilation_ref, row_codes, key_codes)
        pltpu.make_async_copy(held.at[head], held.at[head], in_recv.at[head]).wait()
        attend_head(
            tuple(held.at[head, index] for index in range(4)),
            tuple(made.at[head, index] for index in range(4)),
            row_codes,
            key_codes,
            (keys_t, values_t, keys_sum, values_sum),
        )

        def send_one(step, inner):
            other = lax.rem(me + step, n)
            rows = pl.ds(pl.multiple_of(other * tokens, tokens), tokens)
            for index, target in enumerate(targets):
                pltpu.make_async_remote_copy(
                    src_ref=made.at[head, index, rows, :],
                    dst_ref=target.at[:, columns(me, head)],
                    send_sem=out_send.at[head],
                    recv_sem=out_recv.at[index],
                    device_id={"seq": other},
                    device_id_type=MESH,
                ).start()
            return inner

        for index, target in enumerate(targets):
            pltpu.make_async_copy(
                made.at[head, index, my_rows, :], target.at[:, columns(me, head)], out_recv.at[index]
            ).start()
        lax.fori_loop(1, n, send_one, 0)
        return carry

    lax.fori_loop(0, heads, work_head, 0)

    sent = (n - 1) * tokens

    def finish(head, carry):
        part = held.at[head, :, pl.ds(0, sent), :]
        pltpu.make_async_copy(part, part, in_send.at[head]).wait()
        part = made.at[head, :, pl.ds(0, sent), :]
        pltpu.make_async_copy(part, part, out_send.at[head]).wait()
        return carry

    lax.fori_loop(0, heads, finish, 0)
    for index, target in enumerate(targets):
        pltpu.make_async_copy(target, target, out_recv.at[index]).wait()


def local(queries, keys, values, out_grad, key_blocks, dilation):
    n = lax.axis_size("seq")
    heads = HEADS // n
    tokens, width = queries.shape
    seq = tokens * n
    blocks = key_blocks.shape[1]
    row = jax.ShapeDtypeStruct((tokens, width), jnp.bfloat16)
    anywhere = pl.BlockSpec(memory_space=pl.ANY)
    return pl.pallas_call(
        functools.partial(kernel, n, heads),
        out_shape=(row,) * 4,
        in_specs=[anywhere] * 4
        + [pl.BlockSpec(memory_space=pltpu.VMEM), pl.BlockSpec(memory_space=pltpu.SMEM)],
        out_specs=(anywhere,) * 4,
        scratch_shapes=[
            pltpu.VMEM((heads, 4, seq, HEAD_DIM), jnp.bfloat16),
            pltpu.VMEM((heads, 4, seq, HEAD_DIM), jnp.bfloat16),
            pltpu.VMEM((blocks, seq), jnp.float32),
            pltpu.VMEM((seq, 128), jnp.float32),
            pltpu.VMEM((HEAD_DIM, seq), jnp.bfloat16),
            pltpu.VMEM((HEAD_DIM, seq), jnp.bfloat16),
            pltpu.VMEM((seq, HEAD_DIM), jnp.float32),
            pltpu.VMEM((seq, HEAD_DIM), jnp.float32),
            pltpu.SemaphoreType.DMA((heads,)),
            pltpu.SemaphoreType.DMA((heads,)),
            pltpu.SemaphoreType.DMA((heads,)),
            pltpu.SemaphoreType.DMA((4,)),
        ],
        compiler_params=pltpu.CompilerParams(
            collective_id=0, has_side_effects=True, vmem_limit_bytes=48 * 1024 * 1024
        ),
    )(queries, keys, values, out_grad, key_blocks, dilation)


def solution(mesh):
    rows = P(("batch", "seq"), None)
    return jax.shard_map(
        local,
        mesh=mesh,
        in_specs=(rows, rows, rows, rows, P("batch", None, None), P("batch")),
        out_specs=(rows, rows, rows, rows),
        check_vma=False,
    )
```

```python
import functools
import math

import jax
import jax.numpy as jnp
from jax import lax
from jax.experimental import pallas as pl
from jax.experimental.pallas import tpu as pltpu
from jax.sharding import PartitionSpec as P

HEADS = 32
HEAD_DIM = 128
BLOCK = 64

very_low = -1e30
MESH = pl.DeviceIdType.MESH


def dot(a, b, dims):
    return lax.dot_general(a, b, (dims, ((), ())), preferred_element_type=jnp.float32)


LAST = ((1,), (1,))
PLAIN = ((1,), (0,))
FIRST = ((0,), (0,))


def build_masks(head, lists_ref, dilation_ref, row_codes, key_codes):
    blocks, slots = lists_ref.shape[1], lists_ref.shape[2]
    seq = row_codes.shape[1]
    spacing = dilation_ref[head].astype(jnp.float32)
    inverse = 1.0 / jnp.full((1, 128), spacing, jnp.float32)

    def residue(ids, inv):
        ids = ids.astype(jnp.float32)
        return ids - spacing * jnp.floor((ids + 0.5) * inv)

    lists = lists_ref[head]
    key_ids = lax.broadcasted_iota(jnp.int32, (blocks, blocks), 1)
    member = jnp.zeros((blocks, blocks), jnp.float32)
    for slot in range(slots):
        member = jnp.where(lists[:, slot : slot + 1] == key_ids, 1.0, member)
    spread = (
        lax.broadcasted_iota(jnp.int32, (blocks, seq), 1) // BLOCK
        == lax.broadcasted_iota(jnp.int32, (blocks, seq), 0)
    )
    listed = dot(member, spread.astype(jnp.float32), FIRST)
    query_ids = lax.broadcasted_iota(jnp.int32, (blocks, seq), 1)
    row_codes[...] = jnp.where(listed > 0.5, residue(query_ids, inverse[:, :1]), -1.0)
    key_codes[...] = residue(lax.broadcasted_iota(jnp.int32, (seq, 128), 0), inverse)


def attend_tile(
    start, chunks, diagonal_only, query, grad, key_at, value_at, attended, queries_grad, row_codes, key_codes, scratch
):
    keys_t, values_t, keys_sum, values_sum = scratch
    scale = 1.0 / math.sqrt(HEAD_DIM)
    tile = query.shape[0]
    rows = pl.ds(start, tile)
    chunk = 256
    query_ids = start + lax.broadcasted_iota(jnp.int32, (chunk, tile), 1)
    scores = []
    for c in range(chunks):
        span = slice(c * chunk, (c + 1) * chunk)
        raw = dot(key_at(c), query, LAST)
        codes = key_codes[span, :]
        codes = jnp.concatenate([codes] * (tile // 128), axis=1) if tile > 128 else codes
        first = c * chunk // BLOCK
        wanted = jnp.concatenate(
            [
                jnp.broadcast_to(row_codes[first + b : first + b + 1, rows], (BLOCK, tile))
                for b in range(chunk // BLOCK)
            ],
            axis=0,
        )
        seen = codes == wanted
        if not diagonal_only or c == chunks - 1:
            key_ids = c * chunk + lax.broadcasted_iota(jnp.int32, (chunk, tile), 0)
            seen = seen & (key_ids <= query_ids)
        scores.append(jnp.where(seen, raw, very_low / scale))
    top = functools.reduce(jnp.maximum, [jnp.max(s, axis=0, keepdims=True) for s in scores])
    expos = [jnp.exp2((s - top) * (scale * math.log2(math.e))) for s in scores]
    total = sum(jnp.sum(e, axis=0, keepdims=True) for e in expos)
    share = 1.0 / total
    weights = [e * share for e in expos]
    weights16 = [w.astype(jnp.bfloat16) for w in weights]
    out_t = sum(
        dot(values_t[:, c * chunk : (c + 1) * chunk], weights16[c], PLAIN) for c in range(chunks)
    )
    out16 = jnp.transpose(out_t).astype(jnp.bfloat16)
    attended[...] = out16
    product_t = jnp.transpose(grad.astype(jnp.float32) * out16.astype(jnp.float32))
    delta = jnp.sum(product_t, axis=0, keepdims=True)
    query_t = None
    for c in range(chunks):
        span = slice(c * chunk, (c + 1) * chunk)
        values_sum[span, :] += dot(weights16[c], grad, PLAIN)
        dweights = dot(value_at(c), grad, LAST)
        dscores16 = (weights[c] * (dweights - delta)).astype(jnp.bfloat16)
        keys_sum[span, :] += dot(dscores16, query, PLAIN)
        part = dot(keys_t[:, span], dscores16, PLAIN)
        query_t = part if query_t is None else query_t + part
    queries_grad[...] = jnp.transpose(query_t * scale).astype(jnp.bfloat16)


def turned(rows):
    return jnp.transpose(rows.astype(jnp.float32)).astype(jnp.bfloat16)


def attend_head(ins, outs, row_codes, key_codes, scratch):
    keys_t, values_t, keys_sum, values_sum = scratch
    queries, keys, values, grads = ins
    attended, queries_grad, keys_grad, values_grad = outs
    seq = keys.shape[0]
    keys_t[...] = turned(keys[...])
    values_t[...] = turned(values[...])
    keys_sum[...] = jnp.zeros_like(keys_sum)
    values_sum[...] = jnp.zeros_like(values_sum)

    def one(index, carry):
        start = pl.multiple_of(index * 128, 128)
        rows = pl.ds(start, 128)
        attend_tile(
            start,
            seq // 256,
            False,
            queries[rows, :],
            grads[rows, :],
            lambda c: keys[c * 256 : (c + 1) * 256, :],
            lambda c: values[c * 256 : (c + 1) * 256, :],
            attended.at[rows, :],
            queries_grad.at[rows, :],
            row_codes,
            key_codes,
            scratch,
        )
        return carry

    lax.fori_loop(0, seq // 128, one, 0)
    keys_grad[...] = (keys_sum[...] * (1.0 / math.sqrt(HEAD_DIM))).astype(jnp.bfloat16)
    values_grad[...] = values_sum[...].astype(jnp.bfloat16)


def attend_half(upper, held, low, made, row_codes, key_codes, scratch):
    keys_t, values_t, keys_sum, values_sum = scratch
    half = held.shape[1]
    before = half if upper else 0
    reach = before + half

    def rows_at(index, c):
        if c * 256 < before:
            return low[index - 1, c * 256 : (c + 1) * 256, :]
        return held[index, c * 256 - before : (c + 1) * 256 - before, :]

    for c in range(reach // 256):
        span = slice(c * 256, (c + 1) * 256)
        keys_t[:, span] = turned(rows_at(1, c))
        values_t[:, span] = turned(rows_at(2, c))
    keys_sum[:reach, :] = jnp.zeros((reach, HEAD_DIM), jnp.float32)
    values_sum[:reach, :] = jnp.zeros((reach, HEAD_DIM), jnp.float32)
    for tile in range(half // 256):
        rows = slice(tile * 256, (tile + 1) * 256)
        start = before + tile * 256
        attend_tile(
            start,
            start // 256 + 1,
            True,
            held[0, rows, :],
            held[3, rows, :],
            functools.partial(rows_at, 1),
            functools.partial(rows_at, 2),
            made.at[0, rows, :],
            made.at[1, rows, :],
            row_codes,
            key_codes,
            scratch,
        )


def split_kernel(
    lag,
    relay_lag,
    queries,
    keys,
    values,
    grads,
    lists_ref,
    dilation_ref,
    attended,
    queries_grad,
    keys_grad,
    values_grad,
    held,
    made,
    low_in,
    low_out,
    stage_in,
    stage_out,
    sums,
    row_codes,
    key_codes,
    keys_t,
    values_t,
    keys_sum,
    values_sum,
    held_recv,
    low_recv,
    stage_in_recv,
    stage_out_recv,
    out_recv,
    send,
    low_send,
):
    me = lax.axis_index("seq")
    tokens = queries.shape[0]
    heads = HEADS // 2
    half = 4 * tokens
    side = lax.rem(me, 2)
    plane = me // 2
    across = me + 1 - 2 * side
    along = me + 2 - 4 * lax.rem(plane, 2)
    middle = 6 - 2 * plane + side
    inner = (plane == 1) | (plane == 2)
    sources = (queries, keys, values, grads)
    targets = (attended, queries_grad, keys_grad, values_grad)
    scale = 1.0 / math.sqrt(HEAD_DIM)
    scratch = (keys_t, values_t, keys_sum, values_sum)

    def columns(which, head):
        return pl.ds(pl.multiple_of((which * heads + head) * HEAD_DIM, HEAD_DIM), HEAD_DIM)

    def rows_of(device):
        return pl.ds(pl.multiple_of(lax.rem(device, 4) * tokens, tokens), tokens)

    def push(src, dst, send_sem, recv_sem, device):
        pltpu.make_async_remote_copy(
            src_ref=src,
            dst_ref=dst,
            send_sem=send_sem,
            recv_sem=recv_sem,
            device_id={"seq": device},
            device_id_type=MESH,
        ).start()

    def wait_for(ref, sem):
        pltpu.make_async_copy(ref, ref, sem).wait()

    def loop(count, body):
        def step(k, carry):
            body(k)
            return carry

        lax.fori_loop(0, count, step, 0)

    barrier = pltpu.get_barrier_semaphore()

    def greet(device):
        pl.semaphore_signal(barrier, inc=1, device_id={"seq": device}, device_id_type=MESH)

    def outer_role():
        greet(across)
        greet(along)
        pl.semaphore_wait(barrier, 2)

        def exchange(k):
            for index, source in enumerate(sources):
                push(
                    source.at[:, columns(1 - side, k)],
                    stage_in.at[k, index],
                    send.at[0],
                    stage_in_recv.at[k],
                    across,
                )

        loop(heads, exchange)

        def relay_out(k):
            wait_for(stage_out.at[k], stage_out_recv.at[k])
            for index, target in enumerate(targets):
                push(
                    stage_out.at[k, index],
                    target.at[:, columns(side, k)],
                    send.at[0],
                    out_recv.at[index],
                    across,
                )

        def relay_in(k):
            for index, source in enumerate(sources):
                push(
                    source.at[:, columns(side, k)],
                    held.at[k, index, rows_of(me), :],
                    send.at[0],
                    held_recv.at[k],
                    along,
                )
            wait_for(stage_in.at[k], stage_in_recv.at[k])
            for index in range(4):
                push(
                    stage_in.at[k, index],
                    held.at[k, index, rows_of(across), :],
                    send.at[0],
                    held_recv.at[k],
                    along,
                )

        def both(k):
            relay_in(k)

            @pl.when(k >= relay_lag)
            def _():
                relay_out(k - relay_lag)

        loop(heads, both)
        loop(relay_lag, lambda k: relay_out(heads - relay_lag + k))

    def give(index, k):
        target = targets[index]
        far = rows_of(along + across - me)
        pltpu.make_async_copy(
            made.at[k, index, rows_of(me), :], target.at[:, columns(side, k)], out_recv.at[index]
        ).start()
        push(made.at[k, index, far, :], stage_out.at[k, index], send.at[0], stage_out_recv.at[k], along)
        push(
            made.at[k, index, rows_of(along), :],
            target.at[:, columns(side, k)],
            send.at[0],
            out_recv.at[index],
            along,
        )
        push(
            made.at[k, index, rows_of(across), :],
            target.at[:, columns(side, k)],
            send.at[0],
            out_recv.at[index],
            across,
        )

    def inner_start():
        greet(across)
        greet(along)
        greet(middle)
        pl.semaphore_wait(barrier, 3)

        def exchange(k):
            for index, source in enumerate(sources):
                pltpu.make_async_copy(
                    source.at[:, columns(side, k)],
                    held.at[k, index, rows_of(me), :],
                    held_recv.at[k],
                ).start()
                push(
                    source.at[:, columns(1 - side, k)],
                    held.at[k, index, rows_of(me), :],
                    send.at[0],
                    held_recv.at[k],
                    across,
                )

        loop(heads, exchange)

    def lower_role():
        inner_start()

        def finish(k):
            wait_for(low_in.at[k], low_recv.at[k])
            made[k, 2] = ((sums[k, 0] + low_in[k, 0].astype(jnp.float32)) * scale).astype(jnp.bfloat16)
            made[k, 3] = (sums[k, 1] + low_in[k, 1].astype(jnp.float32)).astype(jnp.bfloat16)
            give(2, k)
            give(3, k)

        def step(k):
            build_masks(side * heads + k, lists_ref, dilation_ref, row_codes, key_codes)
            wait_for(held.at[k], held_recv.at[k])
            push(held.at[k, pl.ds(1, 2)], low_in.at[k], low_send.at[0], low_recv.at[k], middle)
            attend_half(False, held.at[k], None, made.at[k], row_codes, key_codes, scratch)
            give(0, k)
            give(1, k)
            sums[k, 0] = keys_sum[:half, :]
            sums[k, 1] = values_sum[:half, :]

            @pl.when(k >= lag)
            def _():
                finish(k - lag)

        loop(heads, step)
        loop(lag, lambda k: finish(heads - lag + k))

    def upper_role():
        inner_start()

        def step(k):
            build_masks(side * heads + k, lists_ref, dilation_ref, row_codes, key_codes)
            wait_for(held.at[k], held_recv.at[k])
            wait_for(low_in.at[k], low_recv.at[k])
            attend_half(True, held.at[k], low_in.at[k], made.at[k], row_codes, key_codes, scratch)
            low_out[k, 0] = keys_sum[:half, :].astype(jnp.bfloat16)
            low_out[k, 1] = values_sum[:half, :].astype(jnp.bfloat16)
            push(low_out.at[k], low_in.at[k], low_send.at[0], low_recv.at[k], middle)
            made[k, 2] = (keys_sum[half:, :] * scale).astype(jnp.bfloat16)
            made[k, 3] = values_sum[half:, :].astype(jnp.bfloat16)
            for index in range(4):
                give(index, k)

        loop(heads, step)

    pl.when(jnp.logical_not(inner))(outer_role)
    pl.when(plane == 1)(lower_role)
    pl.when(plane == 2)(upper_role)

    wait_for(held, send.at[0])
    pl.when(inner)(lambda: wait_for(low_in, low_send.at[0]))
    for index, target in enumerate(targets):
        wait_for(target, out_recv.at[index])


def kernel(
    n,
    heads,
    queries,
    keys,
    values,
    grads,
    lists_ref,
    dilation_ref,
    attended,
    queries_grad,
    keys_grad,
    values_grad,
    held,
    made,
    row_codes,
    key_codes,
    keys_t,
    values_t,
    keys_sum,
    values_sum,
    in_send,
    in_recv,
    out_send,
    out_recv,
):
    me = lax.axis_index("seq")
    tokens = queries.shape[0]
    sources = (queries, keys, values, grads)
    targets = (attended, queries_grad, keys_grad, values_grad)
    my_rows = pl.ds(pl.multiple_of(me * tokens, tokens), tokens)

    def columns(owner, head):
        return pl.ds(pl.multiple_of((owner * heads + head) * HEAD_DIM, HEAD_DIM), HEAD_DIM)

    barrier = pltpu.get_barrier_semaphore()

    def greet(step, carry):
        pl.semaphore_signal(
            barrier, inc=1, device_id={"seq": lax.rem(me + step, n)}, device_id_type=MESH
        )
        return carry

    lax.fori_loop(1, n, greet, 0)
    pl.semaphore_wait(barrier, n - 1)

    def send_head(head, carry):
        def send_one(step, inner):
            other = lax.rem(me + step, n)
            for index, source in enumerate(sources):
                pltpu.make_async_remote_copy(
                    src_ref=source.at[:, columns(other, head)],
                    dst_ref=held.at[head, index, my_rows, :],
                    send_sem=in_send.at[head],
                    recv_sem=in_recv.at[head],
                    device_id={"seq": other},
                    device_id_type=MESH,
                ).start()
            return inner

        for index, source in enumerate(sources):
            pltpu.make_async_copy(
                source.at[:, columns(me, head)], held.at[head, index, my_rows, :], in_recv.at[head]
            ).start()
        lax.fori_loop(1, n, send_one, 0)
        return carry

    lax.fori_loop(0, heads, send_head, 0)

    def work_head(head, carry):
        build_masks(me * heads + head, lists_ref, dilation_ref, row_codes, key_codes)
        pltpu.make_async_copy(held.at[head], held.at[head], in_recv.at[head]).wait()
        attend_head(
            tuple(held.at[head, index] for index in range(4)),
            tuple(made.at[head, index] for index in range(4)),
            row_codes,
            key_codes,
            (keys_t, values_t, keys_sum, values_sum),
        )

        def send_one(step, inner):
            other = lax.rem(me + step, n)
            rows = pl.ds(pl.multiple_of(other * tokens, tokens), tokens)
            for index, target in enumerate(targets):
                pltpu.make_async_remote_copy(
                    src_ref=made.at[head, index, rows, :],
                    dst_ref=target.at[:, columns(me, head)],
                    send_sem=out_send.at[head],
                    recv_sem=out_recv.at[index],
                    device_id={"seq": other},
                    device_id_type=MESH,
                ).start()
            return inner

        for index, target in enumerate(targets):
            pltpu.make_async_copy(
                made.at[head, index, my_rows, :], target.at[:, columns(me, head)], out_recv.at[index]
            ).start()
        lax.fori_loop(1, n, send_one, 0)
        return carry

    lax.fori_loop(0, heads, work_head, 0)

    sent = (n - 1) * tokens

    def finish(head, carry):
        part = held.at[head, :, pl.ds(0, sent), :]
        pltpu.make_async_copy(part, part, in_send.at[head]).wait()
        part = made.at[head, :, pl.ds(0, sent), :]
        pltpu.make_async_copy(part, part, out_send.at[head]).wait()
        return carry

    lax.fori_loop(0, heads, finish, 0)
    for index, target in enumerate(targets):
        pltpu.make_async_copy(target, target, out_recv.at[index]).wait()


def local(queries, keys, values, out_grad, key_blocks, dilation):
    n = lax.axis_size("seq")
    tokens, width = queries.shape
    seq = tokens * n
    blocks = key_blocks.shape[1]
    row = jax.ShapeDtypeStruct((tokens, width), jnp.bfloat16)
    anywhere = pl.BlockSpec(memory_space=pl.ANY)
    work = [
        pltpu.VMEM((blocks, seq), jnp.float32),
        pltpu.VMEM((seq, 128), jnp.float32),
        pltpu.VMEM((HEAD_DIM, seq), jnp.bfloat16),
        pltpu.VMEM((HEAD_DIM, seq), jnp.bfloat16),
        pltpu.VMEM((seq, HEAD_DIM), jnp.float32),
        pltpu.VMEM((seq, HEAD_DIM), jnp.float32),
    ]
    if n == 8 and tokens % 64 == 0:
        heads = HEADS // 2
        half = seq // 2
        body = functools.partial(split_kernel, 5, 8)
        scratch = [
            pltpu.VMEM((heads, 4, half, HEAD_DIM), jnp.bfloat16),
            pltpu.VMEM((heads, 4, half, HEAD_DIM), jnp.bfloat16),
            pltpu.VMEM((heads, 2, half, HEAD_DIM), jnp.bfloat16),
            pltpu.VMEM((heads, 2, half, HEAD_DIM), jnp.bfloat16),
            pltpu.VMEM((heads, 4, tokens, HEAD_DIM), jnp.bfloat16),
            pltpu.VMEM((heads, 4, tokens, HEAD_DIM), jnp.bfloat16),
            pltpu.VMEM((heads, 2, half, HEAD_DIM), jnp.float32),
            *work,
            pltpu.SemaphoreType.DMA((heads,)),
            pltpu.SemaphoreType.DMA((heads,)),
            pltpu.SemaphoreType.DMA((heads,)),
            pltpu.SemaphoreType.DMA((heads,)),
            pltpu.SemaphoreType.DMA((4,)),
            pltpu.SemaphoreType.DMA((1,)),
            pltpu.SemaphoreType.DMA((1,)),
        ]
    else:
        heads = HEADS // n
        body = functools.partial(kernel, n, heads)
        scratch = [
            pltpu.VMEM((heads, 4, seq, HEAD_DIM), jnp.bfloat16),
            pltpu.VMEM((heads, 4, seq, HEAD_DIM), jnp.bfloat16),
            *work,
            pltpu.SemaphoreType.DMA((heads,)),
            pltpu.SemaphoreType.DMA((heads,)),
            pltpu.SemaphoreType.DMA((heads,)),
            pltpu.SemaphoreType.DMA((4,)),
        ]
    return pl.pallas_call(
        body,
        out_shape=(row,) * 4,
        in_specs=[anywhere] * 4
        + [pl.BlockSpec(memory_space=pltpu.VMEM), pl.BlockSpec(memory_space=pltpu.SMEM)],
        out_specs=(anywhere,) * 4,
        scratch_shapes=scratch,
        compiler_params=pltpu.CompilerParams(
            collective_id=0, has_side_effects=True, vmem_limit_bytes=56 * 1024 * 1024
        ),
    )(queries, keys, values, out_grad, key_blocks, dilation)


def solution(mesh):
    rows = P(("batch", "seq"), None)
    return jax.shard_map(
        local,
        mesh=mesh,
        in_specs=(rows, rows, rows, rows, P("batch", None, None), P("batch")),
        out_specs=(rows, rows, rows, rows),
        check_vma=False,
    )
```

```python
import functools
import math

import jax
import jax.numpy as jnp
from jax import lax
from jax.experimental import pallas as pl
from jax.experimental.pallas import tpu as pltpu
from jax.sharding import PartitionSpec as P

HEADS = 32
HEAD_DIM = 128
BLOCK = 64

very_low = -1e30
MESH = pl.DeviceIdType.MESH


def dot(a, b, dims):
    return lax.dot_general(a, b, (dims, ((), ())), preferred_element_type=jnp.float32)


LAST = ((1,), (1,))
PLAIN = ((1,), (0,))
FIRST = ((0,), (0,))


def build_masks(head, lists_ref, dilation_ref, row_codes, key_codes):
    slots, blocks, count = lists_ref.shape
    seq = row_codes.shape[1]
    spacing = dilation_ref[head].astype(jnp.float32)
    inverse = 1.0 / jnp.full((1, 128), spacing, jnp.float32)

    def residue(ids, inv):
        ids = ids.astype(jnp.float32)
        return ids - spacing * jnp.floor((ids + 0.5) * inv)

    mine = lax.broadcasted_iota(jnp.int32, (blocks, count), 1) == head
    key_ids = lax.broadcasted_iota(jnp.int32, (blocks, blocks), 1)
    member = jnp.zeros((blocks, blocks), jnp.float32)
    for slot in range(slots):
        listed = jnp.sum(jnp.where(mine, lists_ref[slot], 0), axis=1, keepdims=True)
        member = jnp.where(listed == key_ids, 1.0, member)
    spread = (
        lax.broadcasted_iota(jnp.int32, (blocks, seq), 1) // BLOCK
        == lax.broadcasted_iota(jnp.int32, (blocks, seq), 0)
    )
    listed = dot(member, spread.astype(jnp.float32), FIRST)
    query_ids = lax.broadcasted_iota(jnp.int32, (blocks, seq), 1)
    row_codes[...] = jnp.where(listed > 0.5, residue(query_ids, inverse[:, :1]), -1.0)
    key_codes[...] = residue(lax.broadcasted_iota(jnp.int32, (seq, 128), 0), inverse)


def attend_tile(
    start, chunks, diagonal_only, query, grad, key_at, value_at, attended, queries_grad, row_codes, key_codes, scratch
):
    keys_t, values_t, keys_sum, values_sum = scratch
    scale = 1.0 / math.sqrt(HEAD_DIM)
    tile = query.shape[0]
    rows = pl.ds(start, tile)
    chunk = 256
    query_ids = start + lax.broadcasted_iota(jnp.int32, (chunk, tile), 1)
    scores = []
    for c in range(chunks):
        span = slice(c * chunk, (c + 1) * chunk)
        raw = dot(key_at(c), query, LAST)
        codes = key_codes[span, :]
        codes = jnp.concatenate([codes] * (tile // 128), axis=1) if tile > 128 else codes
        first = c * chunk // BLOCK
        wanted = jnp.concatenate(
            [
                jnp.broadcast_to(row_codes[first + b : first + b + 1, rows], (BLOCK, tile))
                for b in range(chunk // BLOCK)
            ],
            axis=0,
        )
        seen = codes == wanted
        if not diagonal_only or c == chunks - 1:
            key_ids = c * chunk + lax.broadcasted_iota(jnp.int32, (chunk, tile), 0)
            seen = seen & (key_ids <= query_ids)
        scores.append(jnp.where(seen, raw, very_low / scale))
    top = functools.reduce(jnp.maximum, [jnp.max(s, axis=0, keepdims=True) for s in scores])
    expos = [jnp.exp2((s - top) * (scale * math.log2(math.e))) for s in scores]
    total = sum(jnp.sum(e, axis=0, keepdims=True) for e in expos)
    share = 1.0 / total
    weights = [e * share for e in expos]
    weights16 = [w.astype(jnp.bfloat16) for w in weights]
    out_t = sum(
        dot(values_t[:, c * chunk : (c + 1) * chunk], weights16[c], PLAIN) for c in range(chunks)
    )
    out16 = jnp.transpose(out_t).astype(jnp.bfloat16)
    attended[...] = out16
    product_t = jnp.transpose(grad.astype(jnp.float32) * out16.astype(jnp.float32))
    delta = jnp.sum(product_t, axis=0, keepdims=True)
    query_t = None
    for c in range(chunks):
        span = slice(c * chunk, (c + 1) * chunk)
        values_sum[span, :] += dot(weights16[c], grad, PLAIN)
        dweights = dot(value_at(c), grad, LAST)
        dscores16 = (weights[c] * (dweights - delta)).astype(jnp.bfloat16)
        keys_sum[span, :] += dot(dscores16, query, PLAIN)
        part = dot(keys_t[:, span], dscores16, PLAIN)
        query_t = part if query_t is None else query_t + part
    queries_grad[...] = jnp.transpose(query_t * scale).astype(jnp.bfloat16)


def turned(rows):
    return jnp.transpose(rows.astype(jnp.float32)).astype(jnp.bfloat16)


def attend_head(ins, outs, row_codes, key_codes, scratch):
    keys_t, values_t, keys_sum, values_sum = scratch
    queries, keys, values, grads = ins
    attended, queries_grad, keys_grad, values_grad = outs
    seq = keys.shape[0]
    keys_t[...] = turned(keys[...])
    values_t[...] = turned(values[...])
    keys_sum[...] = jnp.zeros_like(keys_sum)
    values_sum[...] = jnp.zeros_like(values_sum)

    def one(index, carry):
        start = pl.multiple_of(index * 128, 128)
        rows = pl.ds(start, 128)
        attend_tile(
            start,
            seq // 256,
            False,
            queries[rows, :],
            grads[rows, :],
            lambda c: keys[c * 256 : (c + 1) * 256, :],
            lambda c: values[c * 256 : (c + 1) * 256, :],
            attended.at[rows, :],
            queries_grad.at[rows, :],
            row_codes,
            key_codes,
            scratch,
        )
        return carry

    lax.fori_loop(0, seq // 128, one, 0)
    keys_grad[...] = (keys_sum[...] * (1.0 / math.sqrt(HEAD_DIM))).astype(jnp.bfloat16)
    values_grad[...] = values_sum[...].astype(jnp.bfloat16)


def attend_rows(key_chunks, query_tiles, held, made, row_codes, key_codes, scratch):
    keys_t, values_t, keys_sum, values_sum = scratch

    def rows_at(index, c):
        ref, first = key_chunks[c]
        return ref[index, first : first + 256, :]

    for c in range(len(key_chunks)):
        span = slice(c * 256, (c + 1) * 256)
        keys_t[:, span] = turned(rows_at(0, c))
        values_t[:, span] = turned(rows_at(1, c))
        keys_sum[span, :] = jnp.zeros((256, HEAD_DIM), jnp.float32)
        values_sum[span, :] = jnp.zeros((256, HEAD_DIM), jnp.float32)
    for first, start in query_tiles:
        rows = slice(first, first + 256)
        attend_tile(
            start,
            start // 256 + 1,
            True,
            held[2, rows, :],
            held[3, rows, :],
            functools.partial(rows_at, 0),
            functools.partial(rows_at, 1),
            made.at[0, rows, :],
            made.at[1, rows, :],
            row_codes,
            key_codes,
            scratch,
        )


def split_kernel(
    lag,
    lead,
    queries,
    keys,
    values,
    grads,
    lists_ref,
    dilation_ref,
    attended,
    queries_grad,
    keys_grad,
    values_grad,
    held,
    made,
    low_in,
    low_out,
    stage_out,
    sums,
    row_codes,
    key_codes,
    keys_t,
    values_t,
    keys_sum,
    values_sum,
    pair_recv,
    rest_recv,
    outer_recv,
    low_recv,
    part_recv,
    near_recv,
    stage_recv,
    out_recv,
    send,
    low_send,
):
    me = lax.axis_index("seq")
    tokens = queries.shape[0]
    heads = HEADS // 2
    pair = 2 * tokens
    half = 4 * tokens
    side = lax.rem(me, 2)
    plane = me // 2
    across = me + 1 - 2 * side
    sources = (keys, values, queries, grads)
    targets = (attended, queries_grad, keys_grad, values_grad)
    scale = 1.0 / math.sqrt(HEAD_DIM)
    scratch = (keys_t, values_t, keys_sum, values_sum)

    def at_plane(z):
        return 2 * z + side

    def columns(which, head):
        return pl.ds(pl.multiple_of((which * heads + head) * HEAD_DIM, HEAD_DIM), HEAD_DIM)

    def rows_of(device):
        return pl.ds(pl.multiple_of(lax.rem(device, 4) * tokens, tokens), tokens)

    def push(src, dst, send_sem, recv_sem, device):
        pltpu.make_async_remote_copy(
            src_ref=src,
            dst_ref=dst,
            send_sem=send_sem,
            recv_sem=recv_sem,
            device_id={"seq": device},
            device_id_type=MESH,
        ).start()

    def wait_for(ref, sem):
        pltpu.make_async_copy(ref, ref, sem).wait()

    def loop(count, body):
        def step(k, carry):
            body(k)
            return carry

        lax.fori_loop(0, count, step, 0)

    def enter(*others):
        barrier = pltpu.get_barrier_semaphore()
        for device in others:
            pl.semaphore_signal(barrier, inc=1, device_id={"seq": device}, device_id_type=MESH)
        pl.semaphore_wait(barrier, len(others))

    def arrival(index, k):
        return pair_recv.at[k] if index < 2 else rest_recv.at[k]

    def exchange(keep):
        def body(k):
            for index, source in enumerate(sources):
                if keep:
                    pltpu.make_async_copy(
                        source.at[:, columns(side, k)],
                        held.at[k, index, rows_of(me), :],
                        arrival(index, k),
                    ).start()
                push(
                    source.at[:, columns(1 - side, k)],
                    held.at[k, index, rows_of(me), :],
                    send.at[0],
                    arrival(index, k),
                    across,
                )

        loop(heads, body)

    def masks(k):
        build_masks(side * heads + k, lists_ref, dilation_ref, row_codes, key_codes)

    def give_near(index, k):
        target = targets[index]
        pltpu.make_async_copy(
            made.at[k, index, rows_of(me), :], target.at[:, columns(side, k)], out_recv.at[index]
        ).start()
        push(
            made.at[k, index, rows_of(across), :],
            target.at[:, columns(side, k)],
            send.at[0],
            out_recv.at[index],
            across,
        )

    def run_ahead(forward, step, finish):
        for k in range(lead):
            forward(k)

        def body(k):
            @pl.when(k + lead < heads)
            def _():
                forward(k + lead)

            step(k)

            @pl.when(k >= lag)
            def _():
                finish(k - lag)

        loop(heads, body)
        loop(lag, lambda k: finish(heads - lag + k))

    def add_up(k, rows, extra):
        for index in range(2):
            total = sums[k, index] + low_in[k, index, rows, :].astype(jnp.float32)
            if extra:
                total = total + low_out[k, index, rows, :].astype(jnp.float32)
            made[k, 2 + index, rows, :] = (total * (scale if index == 0 else 1.0)).astype(jnp.bfloat16)
            give_near(2 + index, k)

    def first_role():
        enter(across, at_plane(1), at_plane(2))
        exchange(True)
        rows = slice(0, pair)

        def forward(k):
            wait_for(held.at[k, pl.ds(0, 2), pl.ds(0, pair), :], pair_recv.at[k])
            block = held.at[k, pl.ds(0, 2), pl.ds(0, pair), :]
            push(block, low_in.at[k, :, pl.ds(0, pair), :], send.at[0], low_recv.at[k], at_plane(2))
            push(block, block, send.at[0], outer_recv.at[k], at_plane(1))

        def step(k):
            masks(k)
            wait_for(held.at[k, pl.ds(2, 2), pl.ds(0, pair), :], rest_recv.at[k])
            attend_rows(
                [(held.at[k], 0)], [(0, 0)], held.at[k], made.at[k], row_codes, key_codes, scratch
            )
            give_near(0, k)
            give_near(1, k)
            sums[k, 0] = keys_sum[rows, :]
            sums[k, 1] = values_sum[rows, :]

        def finish(k):
            wait_for(low_in.at[k, :, pl.ds(0, pair), :], part_recv.at[k])
            wait_for(low_out.at[k, :, pl.ds(0, pair), :], near_recv.at[k])
            add_up(k, rows, True)

        run_ahead(forward, step, finish)

    def second_role():
        enter(across, at_plane(0), at_plane(2))
        exchange(True)
        rows = slice(pair, half)

        def forward(k):
            block = held.at[k, pl.ds(0, 2), pl.ds(pair, pair), :]
            wait_for(block, pair_recv.at[k])
            push(block, low_in.at[k, :, pl.ds(pair, pair), :], send.at[0], low_recv.at[k], at_plane(2))

        def step(k):
            masks(k)
            wait_for(held.at[k, pl.ds(2, 2), pl.ds(pair, pair), :], rest_recv.at[k])
            wait_for(held.at[k, pl.ds(0, 2), pl.ds(0, pair), :], outer_recv.at[k])
            attend_rows(
                [(held.at[k], 0), (held.at[k], pair)],
                [(pair, pair)],
                held.at[k],
                made.at[k],
                row_codes,
                key_codes,
                scratch,
            )
            low_out[k, 0, :pair, :] = keys_sum[:pair, :].astype(jnp.bfloat16)
            low_out[k, 1, :pair, :] = values_sum[:pair, :].astype(jnp.bfloat16)
            block = low_out.at[k, :, pl.ds(0, pair), :]
            push(block, block, send.at[0], near_recv.at[k], at_plane(0))
            give_near(0, k)
            give_near(1, k)
            sums[k, 0] = keys_sum[rows, :]
            sums[k, 1] = values_sum[rows, :]

        def finish(k):
            wait_for(low_in.at[k, :, pl.ds(pair, pair), :], part_recv.at[k])
            add_up(k, rows, False)

        run_ahead(forward, step, finish)

    def third_role():
        enter(across, at_plane(0), at_plane(1), at_plane(3))
        exchange(True)

        def step(k):
            masks(k)
            wait_for(held.at[k, pl.ds(0, 2), pl.ds(0, pair), :], pair_recv.at[k])
            wait_for(held.at[k, pl.ds(2, 2), pl.ds(0, pair), :], rest_recv.at[k])
            wait_for(held.at[k, :, pl.ds(pair, pair), :], outer_recv.at[k])
            wait_for(low_in.at[k], low_recv.at[k])
            attend_rows(
                [(low_in.at[k], 0), (low_in.at[k], pair), (held.at[k], 0), (held.at[k], pair)],
                [(0, half), (pair, half + pair)],
                held.at[k],
                made.at[k],
                row_codes,
                key_codes,
                scratch,
            )
            low_out[k, 0] = keys_sum[:half, :].astype(jnp.bfloat16)
            low_out[k, 1] = values_sum[:half, :].astype(jnp.bfloat16)
            for z in range(2):
                block = pl.ds(z * pair, pair)
                push(
                    low_out.at[k, :, block, :],
                    low_in.at[k, :, block, :],
                    low_send.at[0],
                    part_recv.at[k],
                    at_plane(z),
                )
            made[k, 2] = (keys_sum[half:, :] * scale).astype(jnp.bfloat16)
            made[k, 3] = values_sum[half:, :].astype(jnp.bfloat16)
            along = at_plane(3)
            far = rows_of(along + 1 - 2 * side)
            for index, target in enumerate(targets):
                push(made.at[k, index, far, :], stage_out.at[k, index], send.at[0], stage_recv.at[k], along)
                push(
                    made.at[k, index, rows_of(along), :],
                    target.at[:, columns(side, k)],
                    send.at[0],
                    out_recv.at[index],
                    along,
                )
                give_near(index, k)

        loop(heads, step)

    def fourth_role():
        enter(across, at_plane(2))
        exchange(False)

        def forward(k):
            for index, source in enumerate(sources):
                push(
                    source.at[:, columns(side, k)],
                    held.at[k, index, rows_of(me), :],
                    send.at[0],
                    outer_recv.at[k],
                    at_plane(2),
                )
            for first, sem in ((0, pair_recv), (2, rest_recv)):
                block = held.at[k, pl.ds(first, 2), rows_of(across), :]
                wait_for(block, sem.at[k])
                push(block, block, send.at[0], outer_recv.at[k], at_plane(2))

        def finish(k):
            wait_for(stage_out.at[k], stage_recv.at[k])
            for index, target in enumerate(targets):
                push(
                    stage_out.at[k, index],
                    target.at[:, columns(side, k)],
                    send.at[0],
                    out_recv.at[index],
                    across,
                )

        run_ahead(forward, lambda k: None, finish)

    for z, role in enumerate((first_role, second_role, third_role, fourth_role)):
        pl.when(plane == z)(role)

    wait_for(held, send.at[0])
    pl.when(plane == 2)(lambda: wait_for(low_in, low_send.at[0]))
    for index, target in enumerate(targets):
        wait_for(target, out_recv.at[index])


def settle_kernel(pieces, *refs):
    sources, targets, slots, load, store = refs[:4], refs[4:8], refs[8], refs[9], refs[10]
    rows = sources[0].shape[0] // pieces
    loads, stores = [], []
    for index in range(4):
        for piece in range(pieces):
            span = pl.ds(piece * rows, rows)
            number = index * pieces + piece
            loads.append(
                pltpu.make_async_copy(sources[index].at[span, :], slots.at[index, span, :], load.at[number])
            )
            stores.append(
                pltpu.make_async_copy(slots.at[index, span, :], targets[index].at[span, :], store.at[number])
            )
    for copy in loads:
        copy.start()
    for arrived, copy in zip(loads, stores):
        arrived.wait()
        copy.start()
    for copy in stores:
        copy.wait()


def settle(arrays):
    rows, width = arrays[0].shape
    pieces = 4
    anywhere = pl.BlockSpec(memory_space=pl.ANY)
    return pl.pallas_call(
        functools.partial(settle_kernel, pieces),
        out_shape=(jax.ShapeDtypeStruct((rows, width), jnp.bfloat16),) * 4,
        in_specs=[anywhere] * 4,
        out_specs=(anywhere,) * 4,
        scratch_shapes=[
            pltpu.VMEM((4, rows, width), jnp.bfloat16),
            pltpu.SemaphoreType.DMA((4 * pieces,)),
            pltpu.SemaphoreType.DMA((4 * pieces,)),
        ],
        compiler_params=pltpu.CompilerParams(vmem_limit_bytes=56 * 1024 * 1024),
    )(*arrays)


def kernel(
    n,
    heads,
    queries,
    keys,
    values,
    grads,
    lists_ref,
    dilation_ref,
    attended,
    queries_grad,
    keys_grad,
    values_grad,
    held,
    made,
    row_codes,
    key_codes,
    keys_t,
    values_t,
    keys_sum,
    values_sum,
    in_send,
    in_recv,
    out_send,
    out_recv,
):
    me = lax.axis_index("seq")
    tokens = queries.shape[0]
    sources = (queries, keys, values, grads)
    targets = (attended, queries_grad, keys_grad, values_grad)
    my_rows = pl.ds(pl.multiple_of(me * tokens, tokens), tokens)

    def columns(owner, head):
        return pl.ds(pl.multiple_of((owner * heads + head) * HEAD_DIM, HEAD_DIM), HEAD_DIM)

    barrier = pltpu.get_barrier_semaphore()

    def greet(step, carry):
        pl.semaphore_signal(
            barrier, inc=1, device_id={"seq": lax.rem(me + step, n)}, device_id_type=MESH
        )
        return carry

    lax.fori_loop(1, n, greet, 0)
    pl.semaphore_wait(barrier, n - 1)

    def send_head(head, carry):
        def send_one(step, inner):
            other = lax.rem(me + step, n)
            for index, source in enumerate(sources):
                pltpu.make_async_remote_copy(
                    src_ref=source.at[:, columns(other, head)],
                    dst_ref=held.at[head, index, my_rows, :],
                    send_sem=in_send.at[head],
                    recv_sem=in_recv.at[head],
                    device_id={"seq": other},
                    device_id_type=MESH,
                ).start()
            return inner

        for index, source in enumerate(sources):
            pltpu.make_async_copy(
                source.at[:, columns(me, head)], held.at[head, index, my_rows, :], in_recv.at[head]
            ).start()
        lax.fori_loop(1, n, send_one, 0)
        return carry

    lax.fori_loop(0, heads, send_head, 0)

    def work_head(head, carry):
        build_masks(me * heads + head, lists_ref, dilation_ref, row_codes, key_codes)
        pltpu.make_async_copy(held.at[head], held.at[head], in_recv.at[head]).wait()
        attend_head(
            tuple(held.at[head, index] for index in range(4)),
            tuple(made.at[head, index] for index in range(4)),
            row_codes,
            key_codes,
            (keys_t, values_t, keys_sum, values_sum),
        )

        def send_one(step, inner):
            other = lax.rem(me + step, n)
            rows = pl.ds(pl.multiple_of(other * tokens, tokens), tokens)
            for index, target in enumerate(targets):
                pltpu.make_async_remote_copy(
                    src_ref=made.at[head, index, rows, :],
                    dst_ref=target.at[:, columns(me, head)],
                    send_sem=out_send.at[head],
                    recv_sem=out_recv.at[index],
                    device_id={"seq": other},
                    device_id_type=MESH,
                ).start()
            return inner

        for index, target in enumerate(targets):
            pltpu.make_async_copy(
                made.at[head, index, my_rows, :], target.at[:, columns(me, head)], out_recv.at[index]
            ).start()
        lax.fori_loop(1, n, send_one, 0)
        return carry

    lax.fori_loop(0, heads, work_head, 0)

    sent = (n - 1) * tokens

    def finish(head, carry):
        part = held.at[head, :, pl.ds(0, sent), :]
        pltpu.make_async_copy(part, part, in_send.at[head]).wait()
        part = made.at[head, :, pl.ds(0, sent), :]
        pltpu.make_async_copy(part, part, out_send.at[head]).wait()
        return carry

    lax.fori_loop(0, heads, finish, 0)
    for index, target in enumerate(targets):
        pltpu.make_async_copy(target, target, out_recv.at[index]).wait()


def local(queries, keys, values, out_grad, key_blocks, dilation):
    n = lax.axis_size("seq")
    tokens, width = queries.shape
    seq = tokens * n
    blocks = key_blocks.shape[1]
    row = jax.ShapeDtypeStruct((tokens, width), jnp.bfloat16)
    anywhere = pl.BlockSpec(memory_space=pl.ANY)
    work = [
        pltpu.VMEM((blocks, seq), jnp.float32),
        pltpu.VMEM((seq, 128), jnp.float32),
        pltpu.VMEM((HEAD_DIM, seq), jnp.bfloat16),
        pltpu.VMEM((HEAD_DIM, seq), jnp.bfloat16),
        pltpu.VMEM((seq, HEAD_DIM), jnp.float32),
        pltpu.VMEM((seq, HEAD_DIM), jnp.float32),
    ]
    if n == 8 and tokens == 128:
        heads = HEADS // 2
        half = seq // 2
        body = functools.partial(split_kernel, 8, 2)
        scratch = [
            pltpu.VMEM((heads, 4, half, HEAD_DIM), jnp.bfloat16),
            pltpu.VMEM((heads, 4, half, HEAD_DIM), jnp.bfloat16),
            pltpu.VMEM((heads, 2, half, HEAD_DIM), jnp.bfloat16),
            pltpu.VMEM((heads, 2, half, HEAD_DIM), jnp.bfloat16),
            pltpu.VMEM((heads, 4, tokens, HEAD_DIM), jnp.bfloat16),
            pltpu.VMEM((heads, 2, 2 * tokens, HEAD_DIM), jnp.float32),
            *work,
            *[pltpu.SemaphoreType.DMA((heads,))] * 7,
            pltpu.SemaphoreType.DMA((4,)),
            pltpu.SemaphoreType.DMA((1,)),
            pltpu.SemaphoreType.DMA((1,)),
        ]
    else:
        heads = HEADS // n
        body = functools.partial(kernel, n, heads)
        scratch = [
            pltpu.VMEM((heads, 4, seq, HEAD_DIM), jnp.bfloat16),
            pltpu.VMEM((heads, 4, seq, HEAD_DIM), jnp.bfloat16),
            *work,
            pltpu.SemaphoreType.DMA((heads,)),
            pltpu.SemaphoreType.DMA((heads,)),
            pltpu.SemaphoreType.DMA((heads,)),
            pltpu.SemaphoreType.DMA((4,)),
        ]
    results = pl.pallas_call(
        body,
        out_shape=(row,) * 4,
        in_specs=[anywhere] * 4
        + [pl.BlockSpec(memory_space=pltpu.VMEM), pl.BlockSpec(memory_space=pltpu.SMEM)],
        out_specs=(anywhere,) * 4,
        scratch_shapes=scratch,
        compiler_params=pltpu.CompilerParams(
            collective_id=0, has_side_effects=True, vmem_limit_bytes=56 * 1024 * 1024
        ),
    )(queries, keys, values, out_grad, jnp.transpose(key_blocks, (2, 1, 0)), dilation)
    return settle(results)


def solution(mesh):
    rows = P(("batch", "seq"), None)
    return jax.shard_map(
        local,
        mesh=mesh,
        in_specs=(rows, rows, rows, rows, P("batch", None, None), P("batch")),
        out_specs=(rows, rows, rows, rows),
        check_vma=False,
    )
```

```python
import functools
import math

import jax
import jax.numpy as jnp
from jax import lax
from jax.experimental import pallas as pl
from jax.experimental.pallas import tpu as pltpu
from jax.sharding import PartitionSpec as P

HEADS = 32
HEAD_DIM = 128
BLOCK = 64

very_low = -1e30
MESH = pl.DeviceIdType.MESH


def dot(a, b, dims):
    return lax.dot_general(a, b, (dims, ((), ())), preferred_element_type=jnp.float32)


LAST = ((1,), (1,))
PLAIN = ((1,), (0,))
FIRST = ((0,), (0,))


def build_masks(head, lists_ref, dilation_ref, row_codes, key_codes):
    slots, blocks, count = lists_ref.shape
    seq = row_codes.shape[1]
    spacing = dilation_ref[head].astype(jnp.float32)
    inverse = 1.0 / jnp.full((1, 128), spacing, jnp.float32)

    def residue(ids, inv):
        ids = ids.astype(jnp.float32)
        return ids - spacing * jnp.floor((ids + 0.5) * inv)

    mine = lax.broadcasted_iota(jnp.int32, (blocks, count), 1) == head
    key_ids = lax.broadcasted_iota(jnp.int32, (blocks, blocks), 1)
    member = jnp.zeros((blocks, blocks), jnp.float32)
    for slot in range(slots):
        listed = jnp.sum(jnp.where(mine, lists_ref[slot], 0), axis=1, keepdims=True)
        member = jnp.where(listed == key_ids, 1.0, member)
    spread = (
        lax.broadcasted_iota(jnp.int32, (blocks, seq), 1) // BLOCK
        == lax.broadcasted_iota(jnp.int32, (blocks, seq), 0)
    )
    listed = dot(member, spread.astype(jnp.float32), FIRST)
    query_ids = lax.broadcasted_iota(jnp.int32, (blocks, seq), 1)
    row_codes[...] = jnp.where(listed > 0.5, residue(query_ids, inverse[:, :1]), -1.0)
    key_codes[...] = residue(lax.broadcasted_iota(jnp.int32, (seq, 128), 0), inverse)


def attend_tile(
    start, chunks, diagonal_only, query, grad, key_at, value_at, attended, queries_grad, row_codes, key_codes, scratch
):
    keys_t, values_t, keys_sum, values_sum = scratch
    scale = 1.0 / math.sqrt(HEAD_DIM)
    tile = query.shape[0]
    rows = pl.ds(start, tile)
    chunk = 256
    query_ids = start + lax.broadcasted_iota(jnp.int32, (chunk, tile), 1)
    scores = []
    for c in range(chunks):
        span = slice(c * chunk, (c + 1) * chunk)
        raw = dot(key_at(c), query, LAST)
        codes = key_codes[span, :]
        codes = jnp.concatenate([codes] * (tile // 128), axis=1) if tile > 128 else codes
        first = c * chunk // BLOCK
        wanted = jnp.concatenate(
            [
                jnp.broadcast_to(row_codes[first + b : first + b + 1, rows], (BLOCK, tile))
                for b in range(chunk // BLOCK)
            ],
            axis=0,
        )
        seen = codes == wanted
        if not diagonal_only or c == chunks - 1:
            key_ids = c * chunk + lax.broadcasted_iota(jnp.int32, (chunk, tile), 0)
            seen = seen & (key_ids <= query_ids)
        scores.append(jnp.where(seen, raw, very_low / scale))
    top = functools.reduce(jnp.maximum, [jnp.max(s, axis=0, keepdims=True) for s in scores])
    expos = [jnp.exp2((s - top) * (scale * math.log2(math.e))) for s in scores]
    total = sum(jnp.sum(e, axis=0, keepdims=True) for e in expos)
    share = 1.0 / total
    weights = [e * share for e in expos]
    weights16 = [w.astype(jnp.bfloat16) for w in weights]
    out_t = sum(
        dot(values_t[:, c * chunk : (c + 1) * chunk], weights16[c], PLAIN) for c in range(chunks)
    )
    out16 = jnp.transpose(out_t).astype(jnp.bfloat16)
    attended[...] = out16
    product_t = jnp.transpose(grad.astype(jnp.float32) * out16.astype(jnp.float32))
    delta = jnp.sum(product_t, axis=0, keepdims=True)
    query_t = None
    for c in range(chunks):
        span = slice(c * chunk, (c + 1) * chunk)
        values_sum[span, :] += dot(weights16[c], grad, PLAIN)
        dweights = dot(value_at(c), grad, LAST)
        dscores16 = (weights[c] * (dweights - delta)).astype(jnp.bfloat16)
        keys_sum[span, :] += dot(dscores16, query, PLAIN)
        part = dot(keys_t[:, span], dscores16, PLAIN)
        query_t = part if query_t is None else query_t + part
    queries_grad[...] = jnp.transpose(query_t * scale).astype(jnp.bfloat16)


def turned(rows):
    return jnp.transpose(rows.astype(jnp.float32)).astype(jnp.bfloat16)


def attend_head(ins, outs, row_codes, key_codes, scratch):
    keys_t, values_t, keys_sum, values_sum = scratch
    queries, keys, values, grads = ins
    attended, queries_grad, keys_grad, values_grad = outs
    seq = keys.shape[0]
    keys_t[...] = turned(keys[...])
    values_t[...] = turned(values[...])
    keys_sum[...] = jnp.zeros_like(keys_sum)
    values_sum[...] = jnp.zeros_like(values_sum)

    def one(index, carry):
        start = pl.multiple_of(index * 128, 128)
        rows = pl.ds(start, 128)
        attend_tile(
            start,
            seq // 256,
            False,
            queries[rows, :],
            grads[rows, :],
            lambda c: keys[c * 256 : (c + 1) * 256, :],
            lambda c: values[c * 256 : (c + 1) * 256, :],
            attended.at[rows, :],
            queries_grad.at[rows, :],
            row_codes,
            key_codes,
            scratch,
        )
        return carry

    lax.fori_loop(0, seq // 128, one, 0)
    keys_grad[...] = (keys_sum[...] * (1.0 / math.sqrt(HEAD_DIM))).astype(jnp.bfloat16)
    values_grad[...] = values_sum[...].astype(jnp.bfloat16)


def attend_rows(key_chunks, query_tiles, held, made, row_codes, key_codes, scratch):
    keys_t, values_t, keys_sum, values_sum = scratch

    def rows_at(index, c):
        ref, first = key_chunks[c]
        return ref[index, first : first + 256, :]

    for c in range(len(key_chunks)):
        span = slice(c * 256, (c + 1) * 256)
        keys_t[:, span] = turned(rows_at(0, c))
        values_t[:, span] = turned(rows_at(1, c))
        keys_sum[span, :] = jnp.zeros((256, HEAD_DIM), jnp.float32)
        values_sum[span, :] = jnp.zeros((256, HEAD_DIM), jnp.float32)
    for first, start in query_tiles:
        rows = slice(first, first + 256)
        attend_tile(
            start,
            start // 256 + 1,
            True,
            held[2, rows, :],
            held[3, rows, :],
            functools.partial(rows_at, 0),
            functools.partial(rows_at, 1),
            made.at[0, rows, :],
            made.at[1, rows, :],
            row_codes,
            key_codes,
            scratch,
        )


def split_kernel(
    lag,
    lead,
    queries,
    keys,
    values,
    grads,
    lists_ref,
    dilation_ref,
    attended,
    queries_grad,
    keys_grad,
    values_grad,
    held,
    made,
    low_in,
    low_out,
    stage_out,
    sums,
    row_codes,
    key_codes,
    keys_t,
    values_t,
    keys_sum,
    values_sum,
    pair_recv,
    rest_recv,
    outer_recv,
    low_recv,
    part_recv,
    near_recv,
    stage_recv,
    out_recv,
    send,
    low_send,
):
    me = lax.axis_index("seq")
    tokens = queries.shape[0]
    heads = HEADS // 2
    pair = 2 * tokens
    half = 4 * tokens
    side = lax.rem(me, 2)
    plane = me // 2
    across = me + 1 - 2 * side
    sources = (keys, values, queries, grads)
    targets = (attended, queries_grad, keys_grad, values_grad)
    scale = 1.0 / math.sqrt(HEAD_DIM)
    scratch = (keys_t, values_t, keys_sum, values_sum)

    def at_plane(z):
        return 2 * z + side

    def columns(which, head):
        return pl.ds(pl.multiple_of((which * heads + head) * HEAD_DIM, HEAD_DIM), HEAD_DIM)

    def rows_of(device):
        return pl.ds(pl.multiple_of(lax.rem(device, 4) * tokens, tokens), tokens)

    def push(src, dst, send_sem, recv_sem, device):
        pltpu.make_async_remote_copy(
            src_ref=src,
            dst_ref=dst,
            send_sem=send_sem,
            recv_sem=recv_sem,
            device_id={"seq": device},
            device_id_type=MESH,
        ).start()

    def wait_for(ref, sem):
        pltpu.make_async_copy(ref, ref, sem).wait()

    def loop(count, body):
        def step(k, carry):
            body(k)
            return carry

        lax.fori_loop(0, count, step, 0)

    def enter(*others):
        barrier = pltpu.get_barrier_semaphore()
        for device in others:
            pl.semaphore_signal(barrier, inc=1, device_id={"seq": device}, device_id_type=MESH)
        pl.semaphore_wait(barrier, len(others))

    def arrival(index, k):
        return pair_recv.at[k] if index < 2 else rest_recv.at[k]

    def exchange(k, keep=True):
        for index, source in enumerate(sources):
            if keep:
                pltpu.make_async_copy(
                    source.at[:, columns(side, k)],
                    held.at[k, index, rows_of(me), :],
                    arrival(index, k),
                ).start()
            push(
                source.at[:, columns(1 - side, k)],
                held.at[k, index, rows_of(me), :],
                send.at[0],
                arrival(index, k),
                across,
            )

    def masks(k):
        build_masks(side * heads + k, lists_ref, dilation_ref, row_codes, key_codes)

    def give_near(index, k):
        target = targets[index]
        pltpu.make_async_copy(
            made.at[k, index, rows_of(me), :], target.at[:, columns(side, k)], out_recv.at[index]
        ).start()
        push(
            made.at[k, index, rows_of(across), :],
            target.at[:, columns(side, k)],
            send.at[0],
            out_recv.at[index],
            across,
        )

    def run_ahead(stages):
        for lead, body in stages:
            if lead > 0:
                loop(lead, body)

        def step(k):
            for lead, body in stages:
                if lead > 0:
                    pl.when(k + lead < heads)(functools.partial(body, k + lead))
                elif lead < 0:
                    pl.when(k + lead >= 0)(functools.partial(body, k + lead))
                else:
                    body(k)

        loop(heads, step)
        for lead, body in stages:
            if lead < 0:
                loop(-lead, lambda k, lead=lead, body=body: body(heads + lead + k))

    def add_up(k, rows, extra):
        for index in range(2):
            total = sums[k, index] + low_in[k, index, rows, :].astype(jnp.float32)
            if extra:
                total = total + low_out[k, index, rows, :].astype(jnp.float32)
            made[k, 2 + index, rows, :] = (total * (scale if index == 0 else 1.0)).astype(jnp.bfloat16)
            give_near(2 + index, k)

    def first_role():
        enter(across, at_plane(1), at_plane(2))
        rows = slice(0, pair)

        def forward(k):
            wait_for(held.at[k, pl.ds(0, 2), pl.ds(0, pair), :], pair_recv.at[k])
            block = held.at[k, pl.ds(0, 2), pl.ds(0, pair), :]
            push(block, low_in.at[k, :, pl.ds(0, pair), :], send.at[0], low_recv.at[k], at_plane(2))
            push(block, block, send.at[0], outer_recv.at[k], at_plane(1))

        def step(k):
            masks(k)
            wait_for(held.at[k, pl.ds(2, 2), pl.ds(0, pair), :], rest_recv.at[k])
            attend_rows(
                [(held.at[k], 0)], [(0, 0)], held.at[k], made.at[k], row_codes, key_codes, scratch
            )
            give_near(0, k)
            give_near(1, k)
            sums[k, 0] = keys_sum[rows, :]
            sums[k, 1] = values_sum[rows, :]

        def finish(k):
            wait_for(low_in.at[k, :, pl.ds(0, pair), :], part_recv.at[k])
            wait_for(low_out.at[k, :, pl.ds(0, pair), :], near_recv.at[k])
            add_up(k, rows, True)

        run_ahead([(2 * lead, exchange), (lead, forward), (0, step), (-lag, finish)])

    def second_role():
        enter(across, at_plane(0), at_plane(2))
        rows = slice(pair, half)

        def forward(k):
            block = held.at[k, pl.ds(0, 2), pl.ds(pair, pair), :]
            wait_for(block, pair_recv.at[k])
            push(block, low_in.at[k, :, pl.ds(pair, pair), :], send.at[0], low_recv.at[k], at_plane(2))

        def step(k):
            masks(k)
            wait_for(held.at[k, pl.ds(2, 2), pl.ds(pair, pair), :], rest_recv.at[k])
            wait_for(held.at[k, pl.ds(0, 2), pl.ds(0, pair), :], outer_recv.at[k])
            attend_rows(
                [(held.at[k], 0), (held.at[k], pair)],
                [(pair, pair)],
                held.at[k],
                made.at[k],
                row_codes,
                key_codes,
                scratch,
            )
            low_out[k, 0, :pair, :] = keys_sum[:pair, :].astype(jnp.bfloat16)
            low_out[k, 1, :pair, :] = values_sum[:pair, :].astype(jnp.bfloat16)
            block = low_out.at[k, :, pl.ds(0, pair), :]
            push(block, block, send.at[0], near_recv.at[k], at_plane(0))
            give_near(0, k)
            give_near(1, k)
            sums[k, 0] = keys_sum[rows, :]
            sums[k, 1] = values_sum[rows, :]

        def finish(k):
            wait_for(low_in.at[k, :, pl.ds(pair, pair), :], part_recv.at[k])
            add_up(k, rows, False)

        run_ahead([(2 * lead, exchange), (lead, forward), (0, step), (-lag, finish)])

    def third_role():
        enter(across, at_plane(0), at_plane(1), at_plane(3))

        def step(k):
            masks(k)
            wait_for(held.at[k, pl.ds(0, 2), pl.ds(0, pair), :], pair_recv.at[k])
            wait_for(held.at[k, pl.ds(2, 2), pl.ds(0, pair), :], rest_recv.at[k])
            wait_for(held.at[k, :, pl.ds(pair, pair), :], outer_recv.at[k])
            wait_for(low_in.at[k], low_recv.at[k])
            attend_rows(
                [(low_in.at[k], 0), (low_in.at[k], pair), (held.at[k], 0), (held.at[k], pair)],
                [(0, half), (pair, half + pair)],
                held.at[k],
                made.at[k],
                row_codes,
                key_codes,
                scratch,
            )
            low_out[k, 0] = keys_sum[:half, :].astype(jnp.bfloat16)
            low_out[k, 1] = values_sum[:half, :].astype(jnp.bfloat16)
            for z in range(2):
                block = pl.ds(z * pair, pair)
                push(
                    low_out.at[k, :, block, :],
                    low_in.at[k, :, block, :],
                    low_send.at[0],
                    part_recv.at[k],
                    at_plane(z),
                )
            made[k, 2] = (keys_sum[half:, :] * scale).astype(jnp.bfloat16)
            made[k, 3] = values_sum[half:, :].astype(jnp.bfloat16)
            along = at_plane(3)
            far = rows_of(along + 1 - 2 * side)
            for index in range(4):
                push(made.at[k, index, far, :], stage_out.at[k, index], send.at[0], stage_recv.at[k], along)
            for index, target in enumerate(targets):
                push(
                    made.at[k, index, rows_of(along), :],
                    target.at[:, columns(side, k)],
                    send.at[0],
                    out_recv.at[index],
                    along,
                )
                give_near(index, k)

        run_ahead([(2 * lead, exchange), (0, step)])

    def fourth_role():
        enter(across, at_plane(2))

        def own(k):
            for index, source in enumerate(sources):
                push(
                    source.at[:, columns(side, k)],
                    held.at[k, index, rows_of(me), :],
                    send.at[0],
                    outer_recv.at[k],
                    at_plane(2),
                )

        def forward(k):
            for first, sem in ((0, pair_recv), (2, rest_recv)):
                block = held.at[k, pl.ds(first, 2), rows_of(across), :]
                wait_for(block, sem.at[k])
                push(block, block, send.at[0], outer_recv.at[k], at_plane(2))

        def finish(k):
            wait_for(stage_out.at[k], stage_recv.at[k])
            for index, target in enumerate(targets):
                push(
                    stage_out.at[k, index],
                    target.at[:, columns(side, k)],
                    send.at[0],
                    out_recv.at[index],
                    across,
                )

        run_ahead(
            [
                (2 * lead, functools.partial(exchange, keep=False)),
                (lead, own),
                (0, forward),
                (-lag, finish),
            ]
        )

    for z, role in enumerate((first_role, second_role, third_role, fourth_role)):
        pl.when(plane == z)(role)

    wait_for(held, send.at[0])
    pl.when(plane == 2)(lambda: wait_for(low_in, low_send.at[0]))
    for index, target in enumerate(targets):
        wait_for(target, out_recv.at[index])


def settle_kernel(pieces, *refs):
    sources, targets, slots, load, store = refs[:4], refs[4:8], refs[8], refs[9], refs[10]
    rows = sources[0].shape[0] // pieces
    loads, stores = [], []
    for index in range(4):
        for piece in range(pieces):
            span = pl.ds(piece * rows, rows)
            number = index * pieces + piece
            loads.append(
                pltpu.make_async_copy(sources[index].at[span, :], slots.at[index, span, :], load.at[number])
            )
            stores.append(
                pltpu.make_async_copy(slots.at[index, span, :], targets[index].at[span, :], store.at[number])
            )
    for copy in loads:
        copy.start()
    for arrived, copy in zip(loads, stores):
        arrived.wait()
        copy.start()
    for copy in stores:
        copy.wait()


def settle(arrays):
    rows, width = arrays[0].shape
    pieces = 4
    anywhere = pl.BlockSpec(memory_space=pl.ANY)
    return pl.pallas_call(
        functools.partial(settle_kernel, pieces),
        out_shape=(jax.ShapeDtypeStruct((rows, width), jnp.bfloat16),) * 4,
        in_specs=[anywhere] * 4,
        out_specs=(anywhere,) * 4,
        scratch_shapes=[
            pltpu.VMEM((4, rows, width), jnp.bfloat16),
            pltpu.SemaphoreType.DMA((4 * pieces,)),
            pltpu.SemaphoreType.DMA((4 * pieces,)),
        ],
        compiler_params=pltpu.CompilerParams(vmem_limit_bytes=56 * 1024 * 1024),
    )(*arrays)


def kernel(
    n,
    heads,
    queries,
    keys,
    values,
    grads,
    lists_ref,
    dilation_ref,
    attended,
    queries_grad,
    keys_grad,
    values_grad,
    held,
    made,
    row_codes,
    key_codes,
    keys_t,
    values_t,
    keys_sum,
    values_sum,
    in_send,
    in_recv,
    out_send,
    out_recv,
):
    me = lax.axis_index("seq")
    tokens = queries.shape[0]
    sources = (queries, keys, values, grads)
    targets = (attended, queries_grad, keys_grad, values_grad)
    my_rows = pl.ds(pl.multiple_of(me * tokens, tokens), tokens)

    def columns(owner, head):
        return pl.ds(pl.multiple_of((owner * heads + head) * HEAD_DIM, HEAD_DIM), HEAD_DIM)

    barrier = pltpu.get_barrier_semaphore()

    def greet(step, carry):
        pl.semaphore_signal(
            barrier, inc=1, device_id={"seq": lax.rem(me + step, n)}, device_id_type=MESH
        )
        return carry

    lax.fori_loop(1, n, greet, 0)
    pl.semaphore_wait(barrier, n - 1)

    def send_head(head, carry):
        def send_one(step, inner):
            other = lax.rem(me + step, n)
            for index, source in enumerate(sources):
                pltpu.make_async_remote_copy(
                    src_ref=source.at[:, columns(other, head)],
                    dst_ref=held.at[head, index, my_rows, :],
                    send_sem=in_send.at[head],
                    recv_sem=in_recv.at[head],
                    device_id={"seq": other},
                    device_id_type=MESH,
                ).start()
            return inner

        for index, source in enumerate(sources):
            pltpu.make_async_copy(
                source.at[:, columns(me, head)], held.at[head, index, my_rows, :], in_recv.at[head]
            ).start()
        lax.fori_loop(1, n, send_one, 0)
        return carry

    lax.fori_loop(0, heads, send_head, 0)

    def work_head(head, carry):
        build_masks(me * heads + head, lists_ref, dilation_ref, row_codes, key_codes)
        pltpu.make_async_copy(held.at[head], held.at[head], in_recv.at[head]).wait()
        attend_head(
            tuple(held.at[head, index] for index in range(4)),
            tuple(made.at[head, index] for index in range(4)),
            row_codes,
            key_codes,
            (keys_t, values_t, keys_sum, values_sum),
        )

        def send_one(step, inner):
            other = lax.rem(me + step, n)
            rows = pl.ds(pl.multiple_of(other * tokens, tokens), tokens)
            for index, target in enumerate(targets):
                pltpu.make_async_remote_copy(
                    src_ref=made.at[head, index, rows, :],
                    dst_ref=target.at[:, columns(me, head)],
                    send_sem=out_send.at[head],
                    recv_sem=out_recv.at[index],
                    device_id={"seq": other},
                    device_id_type=MESH,
                ).start()
            return inner

        for index, target in enumerate(targets):
            pltpu.make_async_copy(
                made.at[head, index, my_rows, :], target.at[:, columns(me, head)], out_recv.at[index]
            ).start()
        lax.fori_loop(1, n, send_one, 0)
        return carry

    lax.fori_loop(0, heads, work_head, 0)

    sent = (n - 1) * tokens

    def finish(head, carry):
        part = held.at[head, :, pl.ds(0, sent), :]
        pltpu.make_async_copy(part, part, in_send.at[head]).wait()
        part = made.at[head, :, pl.ds(0, sent), :]
        pltpu.make_async_copy(part, part, out_send.at[head]).wait()
        return carry

    lax.fori_loop(0, heads, finish, 0)
    for index, target in enumerate(targets):
        pltpu.make_async_copy(target, target, out_recv.at[index]).wait()


def local(queries, keys, values, out_grad, key_blocks, dilation):
    n = lax.axis_size("seq")
    tokens, width = queries.shape
    seq = tokens * n
    blocks = key_blocks.shape[1]
    row = jax.ShapeDtypeStruct((tokens, width), jnp.bfloat16)
    anywhere = pl.BlockSpec(memory_space=pl.ANY)
    work = [
        pltpu.VMEM((blocks, seq), jnp.float32),
        pltpu.VMEM((seq, 128), jnp.float32),
        pltpu.VMEM((HEAD_DIM, seq), jnp.bfloat16),
        pltpu.VMEM((HEAD_DIM, seq), jnp.bfloat16),
        pltpu.VMEM((seq, HEAD_DIM), jnp.float32),
        pltpu.VMEM((seq, HEAD_DIM), jnp.float32),
    ]
    if n == 8 and tokens == 128:
        heads = HEADS // 2
        half = seq // 2
        body = functools.partial(split_kernel, 8, 2)
        scratch = [
            pltpu.VMEM((heads, 4, half, HEAD_DIM), jnp.bfloat16),
            pltpu.VMEM((heads, 4, half, HEAD_DIM), jnp.bfloat16),
            pltpu.VMEM((heads, 2, half, HEAD_DIM), jnp.bfloat16),
            pltpu.VMEM((heads, 2, half, HEAD_DIM), jnp.bfloat16),
            pltpu.VMEM((heads, 4, tokens, HEAD_DIM), jnp.bfloat16),
            pltpu.VMEM((heads, 2, 2 * tokens, HEAD_DIM), jnp.float32),
            *work,
            *[pltpu.SemaphoreType.DMA((heads,))] * 7,
            pltpu.SemaphoreType.DMA((4,)),
            pltpu.SemaphoreType.DMA((1,)),
            pltpu.SemaphoreType.DMA((1,)),
        ]
    else:
        heads = HEADS // n
        body = functools.partial(kernel, n, heads)
        scratch = [
            pltpu.VMEM((heads, 4, seq, HEAD_DIM), jnp.bfloat16),
            pltpu.VMEM((heads, 4, seq, HEAD_DIM), jnp.bfloat16),
            *work,
            pltpu.SemaphoreType.DMA((heads,)),
            pltpu.SemaphoreType.DMA((heads,)),
            pltpu.SemaphoreType.DMA((heads,)),
            pltpu.SemaphoreType.DMA((4,)),
        ]
    results = pl.pallas_call(
        body,
        out_shape=(row,) * 4,
        in_specs=[anywhere] * 4
        + [pl.BlockSpec(memory_space=pltpu.VMEM), pl.BlockSpec(memory_space=pltpu.SMEM)],
        out_specs=(anywhere,) * 4,
        scratch_shapes=scratch,
        compiler_params=pltpu.CompilerParams(
            collective_id=0, has_side_effects=True, vmem_limit_bytes=56 * 1024 * 1024
        ),
    )(queries, keys, values, out_grad, jnp.transpose(key_blocks, (2, 1, 0)), dilation)
    return settle(results)


def solution(mesh):
    rows = P(("batch", "seq"), None)
    return jax.shard_map(
        local,
        mesh=mesh,
        in_specs=(rows, rows, rows, rows, P("batch", None, None), P("batch")),
        out_specs=(rows, rows, rows, rows),
        check_vma=False,
    )
```

```python
import functools
import math

import jax
import jax.numpy as jnp
from jax import lax
from jax.experimental import pallas as pl
from jax.experimental.pallas import tpu as pltpu
from jax.sharding import PartitionSpec as P

HEADS = 32
HEAD_DIM = 128
BLOCK = 64

very_low = -1e30
MESH = pl.DeviceIdType.MESH


def dot(a, b, dims):
    return lax.dot_general(a, b, (dims, ((), ())), preferred_element_type=jnp.float32)


LAST = ((1,), (1,))
PLAIN = ((1,), (0,))
FIRST = ((0,), (0,))


def build_masks(head, lists_ref, dilation_ref, row_codes, key_codes):
    slots, blocks, count = lists_ref.shape
    seq = row_codes.shape[1]
    spacing = dilation_ref[head].astype(jnp.float32)
    inverse = 1.0 / jnp.full((1, 128), spacing, jnp.float32)

    def residue(ids, inv):
        ids = ids.astype(jnp.float32)
        return ids - spacing * jnp.floor((ids + 0.5) * inv)

    mine = lax.broadcasted_iota(jnp.int32, (blocks, count), 1) == head
    key_ids = lax.broadcasted_iota(jnp.int32, (blocks, blocks), 1)
    member = jnp.zeros((blocks, blocks), jnp.float32)
    for slot in range(slots):
        listed = jnp.sum(jnp.where(mine, lists_ref[slot], 0), axis=1, keepdims=True)
        member = jnp.where(listed == key_ids, 1.0, member)
    spread = (
        lax.broadcasted_iota(jnp.int32, (blocks, seq), 1) // BLOCK
        == lax.broadcasted_iota(jnp.int32, (blocks, seq), 0)
    )
    listed = dot(member, spread.astype(jnp.float32), FIRST)
    query_ids = lax.broadcasted_iota(jnp.int32, (blocks, seq), 1)
    row_codes[...] = jnp.where(listed > 0.5, residue(query_ids, inverse[:, :1]), -1.0)
    key_codes[...] = residue(lax.broadcasted_iota(jnp.int32, (seq, 128), 0), inverse)


def attend_tile(
    start, chunks, diagonal_only, fresh, query, grad, key_at, value_at, attended, queries_grad, row_codes, key_codes, scratch
):
    keys_t, values_t, keys_sum, values_sum = scratch
    scale = 1.0 / math.sqrt(HEAD_DIM)
    tile = query.shape[0]
    rows = pl.ds(start, tile)
    chunk = 256
    query_ids = start + lax.broadcasted_iota(jnp.int32, (chunk, tile), 1)
    scores = []
    for c in range(chunks):
        span = slice(c * chunk, (c + 1) * chunk)
        raw = dot(key_at(c), query, LAST)
        codes = key_codes[span, :]
        codes = jnp.concatenate([codes] * (tile // 128), axis=1) if tile > 128 else codes
        first = c * chunk // BLOCK
        wanted = jnp.concatenate(
            [
                jnp.broadcast_to(row_codes[first + b : first + b + 1, rows], (BLOCK, tile))
                for b in range(chunk // BLOCK)
            ],
            axis=0,
        )
        seen = codes == wanted
        if not diagonal_only or c == chunks - 1:
            key_ids = c * chunk + lax.broadcasted_iota(jnp.int32, (chunk, tile), 0)
            seen = seen & (key_ids <= query_ids)
        scores.append(jnp.where(seen, raw, very_low / scale))
    top = functools.reduce(jnp.maximum, [jnp.max(s, axis=0, keepdims=True) for s in scores])
    yield
    expos, dweights = [], []
    for c in range(chunks):
        dweights.append(dot(value_at(c), grad, LAST))
        expos.append(jnp.exp2((scores[c] - top) * (scale * math.log2(math.e))))
    total = sum(jnp.sum(e, axis=0, keepdims=True) for e in expos)
    share = 1.0 / total
    grad_t = turned(grad).astype(jnp.float32)
    yield
    weights, out_t = [], None
    for c in range(chunks):
        span = slice(c * chunk, (c + 1) * chunk)
        weights.append(expos[c] * share)
        weights16 = weights[c].astype(jnp.bfloat16)
        part = dot(values_t[:, span], weights16, PLAIN)
        out_t = part if out_t is None else out_t + part
        part = dot(weights16, grad, PLAIN)
        values_sum[span, :] = part if fresh else values_sum[span, :] + part
    out16_t = out_t.astype(jnp.bfloat16)
    attended[...] = jnp.transpose(out16_t)
    delta = jnp.sum(grad_t * out16_t.astype(jnp.float32), axis=0, keepdims=True)
    yield
    query_t = None
    for c in range(chunks):
        span = slice(c * chunk, (c + 1) * chunk)
        dscores16 = (weights[c] * (dweights[c] - delta)).astype(jnp.bfloat16)
        part = dot(dscores16, query, PLAIN)
        keys_sum[span, :] = part if fresh else keys_sum[span, :] + part
        part = dot(keys_t[:, span], dscores16, PLAIN)
        query_t = part if query_t is None else query_t + part
    queries_grad[...] = jnp.transpose((query_t * scale).astype(jnp.bfloat16))
    yield


def turned(rows):
    return jnp.transpose(rows)


def attend_head(ins, outs, row_codes, key_codes, scratch):
    keys_t, values_t, keys_sum, values_sum = scratch
    queries, keys, values, grads = ins
    attended, queries_grad, keys_grad, values_grad = outs
    seq = keys.shape[0]
    keys_t[...] = turned(keys[...])
    values_t[...] = turned(values[...])
    keys_sum[...] = jnp.zeros_like(keys_sum)
    values_sum[...] = jnp.zeros_like(values_sum)

    def one(index, carry):
        start = pl.multiple_of(index * 128, 128)
        rows = pl.ds(start, 128)
        phases = attend_tile(
            start,
            seq // 256,
            False,
            False,
            queries[rows, :],
            grads[rows, :],
            lambda c: keys[c * 256 : (c + 1) * 256, :],
            lambda c: values[c * 256 : (c + 1) * 256, :],
            attended.at[rows, :],
            queries_grad.at[rows, :],
            row_codes,
            key_codes,
            scratch,
        )
        for _ in phases:
            pass
        return carry

    lax.fori_loop(0, seq // 128, one, 0)
    keys_grad[...] = (keys_sum[...] * (1.0 / math.sqrt(HEAD_DIM))).astype(jnp.bfloat16)
    values_grad[...] = values_sum[...].astype(jnp.bfloat16)


def attend_rows(key_chunks, query_tiles, held, made, row_codes, key_codes, scratch):
    keys_t, values_t, keys_sum, values_sum = scratch

    def rows_at(index, c):
        ref, first = key_chunks[c]
        return ref[index, first : first + 256, :]

    for c in range(len(key_chunks)):
        span = slice(c * 256, (c + 1) * 256)
        keys_t[:, span] = turned(rows_at(0, c))
        values_t[:, span] = turned(rows_at(1, c))
    tiles = []
    for number, (first, start) in enumerate(query_tiles):
        rows = slice(first, first + 256)
        phases = attend_tile(
            start,
            start // 256 + 1,
            True,
            number == 0,
            held[2, rows, :],
            held[3, rows, :],
            functools.partial(rows_at, 0),
            functools.partial(rows_at, 1),
            made.at[0, rows, :],
            made.at[1, rows, :],
            row_codes,
            key_codes,
            scratch,
        )
        tiles.append(phases)
    for _ in zip(*tiles):
        pass


def split_kernel(
    lag,
    lead,
    queries,
    keys,
    values,
    grads,
    lists_ref,
    dilation_ref,
    attended,
    queries_grad,
    keys_grad,
    values_grad,
    held,
    made,
    low_in,
    low_out,
    stage_out,
    sums,
    row_codes,
    key_codes,
    keys_t,
    values_t,
    keys_sum,
    values_sum,
    pair_recv,
    rest_recv,
    outer_recv,
    low_recv,
    part_recv,
    near_recv,
    stage_recv,
    out_recv,
    send,
    low_send,
):
    me = lax.axis_index("seq")
    tokens = queries.shape[0]
    heads = HEADS // 2
    pair = 2 * tokens
    half = 4 * tokens
    side = lax.rem(me, 2)
    plane = me // 2
    across = me + 1 - 2 * side
    sources = (keys, values, queries, grads)
    targets = (attended, queries_grad, keys_grad, values_grad)
    scale = 1.0 / math.sqrt(HEAD_DIM)
    scratch = (keys_t, values_t, keys_sum, values_sum)

    def at_plane(z):
        return 2 * z + side

    def columns(which, head):
        return pl.ds(pl.multiple_of((which * heads + head) * HEAD_DIM, HEAD_DIM), HEAD_DIM)

    def rows_of(device):
        return pl.ds(pl.multiple_of(lax.rem(device, 4) * tokens, tokens), tokens)

    def push(src, dst, send_sem, recv_sem, device):
        pltpu.make_async_remote_copy(
            src_ref=src,
            dst_ref=dst,
            send_sem=send_sem,
            recv_sem=recv_sem,
            device_id={"seq": device},
            device_id_type=MESH,
        ).start()

    def wait_for(ref, sem):
        pltpu.make_async_copy(ref, ref, sem).wait()

    def loop(count, body):
        def step(k, carry):
            body(k)
            return carry

        lax.fori_loop(0, count, step, 0)

    def enter(*others):
        barrier = pltpu.get_barrier_semaphore()
        for device in others:
            pl.semaphore_signal(barrier, inc=1, device_id={"seq": device}, device_id_type=MESH)
        pl.semaphore_wait(barrier, len(others))

    def arrival(index, k):
        return pair_recv.at[k] if index < 2 else rest_recv.at[k]

    def exchange(k, keep=True):
        for index, source in enumerate(sources):
            if keep:
                pltpu.make_async_copy(
                    source.at[:, columns(side, k)],
                    held.at[k, index, rows_of(me), :],
                    arrival(index, k),
                ).start()
            push(
                source.at[:, columns(1 - side, k)],
                held.at[k, index, rows_of(me), :],
                send.at[0],
                arrival(index, k),
                across,
            )

    def masks(k):
        build_masks(side * heads + k, lists_ref, dilation_ref, row_codes, key_codes)

    def give_near(index, k):
        target = targets[index]
        pltpu.make_async_copy(
            made.at[k, index, rows_of(me), :], target.at[:, columns(side, k)], out_recv.at[index]
        ).start()
        push(
            made.at[k, index, rows_of(across), :],
            target.at[:, columns(side, k)],
            send.at[0],
            out_recv.at[index],
            across,
        )

    def run_ahead(stages):
        for lead, body in stages:
            if lead > 0:
                loop(lead, body)

        def step(k):
            for lead, body in stages:
                if lead > 0:
                    pl.when(k + lead < heads)(functools.partial(body, k + lead))
                elif lead < 0:
                    pl.when(k + lead >= 0)(functools.partial(body, k + lead))
                else:
                    body(k)

        loop(heads, step)
        for lead, body in stages:
            if lead < 0:
                loop(-lead, lambda k, lead=lead, body=body: body(heads + lead + k))

    def add_up(k, rows, extra):
        for index in range(2):
            total = sums[k, index] + low_in[k, index, rows, :].astype(jnp.float32)
            if extra:
                total = total + low_out[k, index, rows, :].astype(jnp.float32)
            made[k, 2 + index, rows, :] = (total * (scale if index == 0 else 1.0)).astype(jnp.bfloat16)
            give_near(2 + index, k)

    def first_role():
        enter(across, at_plane(1), at_plane(2))
        rows = slice(0, pair)

        def forward(k):
            wait_for(held.at[k, pl.ds(0, 2), pl.ds(0, pair), :], pair_recv.at[k])
            block = held.at[k, pl.ds(0, 2), pl.ds(0, pair), :]
            push(block, low_in.at[k, :, pl.ds(0, pair), :], send.at[0], low_recv.at[k], at_plane(2))
            push(block, block, send.at[0], outer_recv.at[k], at_plane(1))

        def step(k):
            masks(k)
            wait_for(held.at[k, pl.ds(2, 2), pl.ds(0, pair), :], rest_recv.at[k])
            attend_rows(
                [(held.at[k], 0)], [(0, 0)], held.at[k], made.at[k], row_codes, key_codes, scratch
            )
            give_near(0, k)
            give_near(1, k)
            sums[k, 0] = keys_sum[rows, :]
            sums[k, 1] = values_sum[rows, :]

        def finish(k):
            wait_for(low_in.at[k, :, pl.ds(0, pair), :], part_recv.at[k])
            wait_for(low_out.at[k, :, pl.ds(0, pair), :], near_recv.at[k])
            add_up(k, rows, True)

        run_ahead([(2 * lead, exchange), (lead, forward), (0, step), (-lag, finish)])

    def second_role():
        enter(across, at_plane(0), at_plane(2))
        rows = slice(pair, half)

        def forward(k):
            block = held.at[k, pl.ds(0, 2), pl.ds(pair, pair), :]
            wait_for(block, pair_recv.at[k])
            push(block, low_in.at[k, :, pl.ds(pair, pair), :], send.at[0], low_recv.at[k], at_plane(2))

        def step(k):
            masks(k)
            wait_for(held.at[k, pl.ds(2, 2), pl.ds(pair, pair), :], rest_recv.at[k])
            wait_for(held.at[k, pl.ds(0, 2), pl.ds(0, pair), :], outer_recv.at[k])
            attend_rows(
                [(held.at[k], 0), (held.at[k], pair)],
                [(pair, pair)],
                held.at[k],
                made.at[k],
                row_codes,
                key_codes,
                scratch,
            )
            low_out[k, 0, :pair, :] = keys_sum[:pair, :].astype(jnp.bfloat16)
            low_out[k, 1, :pair, :] = values_sum[:pair, :].astype(jnp.bfloat16)
            block = low_out.at[k, :, pl.ds(0, pair), :]
            push(block, block, send.at[0], near_recv.at[k], at_plane(0))
            give_near(0, k)
            give_near(1, k)
            sums[k, 0] = keys_sum[rows, :]
            sums[k, 1] = values_sum[rows, :]

        def finish(k):
            wait_for(low_in.at[k, :, pl.ds(pair, pair), :], part_recv.at[k])
            add_up(k, rows, False)

        run_ahead([(2 * lead, exchange), (lead, forward), (0, step), (-lag, finish)])

    def third_role():
        enter(across, at_plane(0), at_plane(1), at_plane(3))

        def step(k):
            masks(k)
            wait_for(held.at[k, pl.ds(0, 2), pl.ds(0, pair), :], pair_recv.at[k])
            wait_for(held.at[k, pl.ds(2, 2), pl.ds(0, pair), :], rest_recv.at[k])
            wait_for(held.at[k, :, pl.ds(pair, pair), :], outer_recv.at[k])
            wait_for(low_in.at[k], low_recv.at[k])
            attend_rows(
                [(low_in.at[k], 0), (low_in.at[k], pair), (held.at[k], 0), (held.at[k], pair)],
                [(pair, half + pair), (0, half)],
                held.at[k],
                made.at[k],
                row_codes,
                key_codes,
                scratch,
            )
            low_out[k, 0] = keys_sum[:half, :].astype(jnp.bfloat16)
            low_out[k, 1] = values_sum[:half, :].astype(jnp.bfloat16)
            for z in range(2):
                block = pl.ds(z * pair, pair)
                push(
                    low_out.at[k, :, block, :],
                    low_in.at[k, :, block, :],
                    low_send.at[0],
                    part_recv.at[k],
                    at_plane(z),
                )
            made[k, 2] = (keys_sum[half:, :] * scale).astype(jnp.bfloat16)
            made[k, 3] = values_sum[half:, :].astype(jnp.bfloat16)
            along = at_plane(3)
            far = rows_of(along + 1 - 2 * side)
            for index in range(4):
                push(made.at[k, index, far, :], stage_out.at[k, index], send.at[0], stage_recv.at[k], along)
            for index, target in enumerate(targets):
                push(
                    made.at[k, index, rows_of(along), :],
                    target.at[:, columns(side, k)],
                    send.at[0],
                    out_recv.at[index],
                    along,
                )
                give_near(index, k)

        run_ahead([(2 * lead, exchange), (0, step)])

    def fourth_role():
        enter(across, at_plane(2))

        def own(k):
            for index, source in enumerate(sources):
                push(
                    source.at[:, columns(side, k)],
                    held.at[k, index, rows_of(me), :],
                    send.at[0],
                    outer_recv.at[k],
                    at_plane(2),
                )

        def forward(k):
            for first, sem in ((0, pair_recv), (2, rest_recv)):
                block = held.at[k, pl.ds(first, 2), rows_of(across), :]
                wait_for(block, sem.at[k])
                push(block, block, send.at[0], outer_recv.at[k], at_plane(2))

        def finish(k):
            wait_for(stage_out.at[k], stage_recv.at[k])
            for index, target in enumerate(targets):
                push(
                    stage_out.at[k, index],
                    target.at[:, columns(side, k)],
                    send.at[0],
                    out_recv.at[index],
                    across,
                )

        run_ahead(
            [
                (2 * lead, functools.partial(exchange, keep=False)),
                (lead, own),
                (0, forward),
                (-lag, finish),
            ]
        )

    for z, role in enumerate((first_role, second_role, third_role, fourth_role)):
        pl.when(plane == z)(role)

    wait_for(held, send.at[0])
    pl.when(plane == 2)(lambda: wait_for(low_in, low_send.at[0]))
    for index, target in enumerate(targets):
        wait_for(target, out_recv.at[index])


def settle_kernel(pieces, *refs):
    sources, targets, slots, load, store = refs[:4], refs[4:8], refs[8], refs[9], refs[10]
    rows = sources[0].shape[0] // pieces
    loads, stores = [], []
    for index in range(4):
        for piece in range(pieces):
            span = pl.ds(piece * rows, rows)
            number = index * pieces + piece
            loads.append(
                pltpu.make_async_copy(sources[index].at[span, :], slots.at[index, span, :], load.at[number])
            )
            stores.append(
                pltpu.make_async_copy(slots.at[index, span, :], targets[index].at[span, :], store.at[number])
            )
    for copy in loads:
        copy.start()
    for arrived, copy in zip(loads, stores):
        arrived.wait()
        copy.start()
    for copy in stores:
        copy.wait()


def settle(arrays):
    rows, width = arrays[0].shape
    pieces = 4
    anywhere = pl.BlockSpec(memory_space=pl.ANY)
    return pl.pallas_call(
        functools.partial(settle_kernel, pieces),
        out_shape=(jax.ShapeDtypeStruct((rows, width), jnp.bfloat16),) * 4,
        in_specs=[anywhere] * 4,
        out_specs=(anywhere,) * 4,
        scratch_shapes=[
            pltpu.VMEM((4, rows, width), jnp.bfloat16),
            pltpu.SemaphoreType.DMA((4 * pieces,)),
            pltpu.SemaphoreType.DMA((4 * pieces,)),
        ],
        compiler_params=pltpu.CompilerParams(vmem_limit_bytes=56 * 1024 * 1024),
    )(*arrays)


def kernel(
    n,
    heads,
    queries,
    keys,
    values,
    grads,
    lists_ref,
    dilation_ref,
    attended,
    queries_grad,
    keys_grad,
    values_grad,
    held,
    made,
    row_codes,
    key_codes,
    keys_t,
    values_t,
    keys_sum,
    values_sum,
    in_send,
    in_recv,
    out_send,
    out_recv,
):
    me = lax.axis_index("seq")
    tokens = queries.shape[0]
    sources = (queries, keys, values, grads)
    targets = (attended, queries_grad, keys_grad, values_grad)
    my_rows = pl.ds(pl.multiple_of(me * tokens, tokens), tokens)

    def columns(owner, head):
        return pl.ds(pl.multiple_of((owner * heads + head) * HEAD_DIM, HEAD_DIM), HEAD_DIM)

    barrier = pltpu.get_barrier_semaphore()

    def greet(step, carry):
        pl.semaphore_signal(
            barrier, inc=1, device_id={"seq": lax.rem(me + step, n)}, device_id_type=MESH
        )
        return carry

    lax.fori_loop(1, n, greet, 0)
    pl.semaphore_wait(barrier, n - 1)

    def send_head(head, carry):
        def send_one(step, inner):
            other = lax.rem(me + step, n)
            for index, source in enumerate(sources):
                pltpu.make_async_remote_copy(
                    src_ref=source.at[:, columns(other, head)],
                    dst_ref=held.at[head, index, my_rows, :],
                    send_sem=in_send.at[head],
                    recv_sem=in_recv.at[head],
                    device_id={"seq": other},
                    device_id_type=MESH,
                ).start()
            return inner

        for index, source in enumerate(sources):
            pltpu.make_async_copy(
                source.at[:, columns(me, head)], held.at[head, index, my_rows, :], in_recv.at[head]
            ).start()
        lax.fori_loop(1, n, send_one, 0)
        return carry

    lax.fori_loop(0, heads, send_head, 0)

    def work_head(head, carry):
        build_masks(me * heads + head, lists_ref, dilation_ref, row_codes, key_codes)
        pltpu.make_async_copy(held.at[head], held.at[head], in_recv.at[head]).wait()
        attend_head(
            tuple(held.at[head, index] for index in range(4)),
            tuple(made.at[head, index] for index in range(4)),
            row_codes,
            key_codes,
            (keys_t, values_t, keys_sum, values_sum),
        )

        def send_one(step, inner):
            other = lax.rem(me + step, n)
            rows = pl.ds(pl.multiple_of(other * tokens, tokens), tokens)
            for index, target in enumerate(targets):
                pltpu.make_async_remote_copy(
                    src_ref=made.at[head, index, rows, :],
                    dst_ref=target.at[:, columns(me, head)],
                    send_sem=out_send.at[head],
                    recv_sem=out_recv.at[index],
                    device_id={"seq": other},
                    device_id_type=MESH,
                ).start()
            return inner

        for index, target in enumerate(targets):
            pltpu.make_async_copy(
                made.at[head, index, my_rows, :], target.at[:, columns(me, head)], out_recv.at[index]
            ).start()
        lax.fori_loop(1, n, send_one, 0)
        return carry

    lax.fori_loop(0, heads, work_head, 0)

    sent = (n - 1) * tokens

    def finish(head, carry):
        part = held.at[head, :, pl.ds(0, sent), :]
        pltpu.make_async_copy(part, part, in_send.at[head]).wait()
        part = made.at[head, :, pl.ds(0, sent), :]
        pltpu.make_async_copy(part, part, out_send.at[head]).wait()
        return carry

    lax.fori_loop(0, heads, finish, 0)
    for index, target in enumerate(targets):
        pltpu.make_async_copy(target, target, out_recv.at[index]).wait()


def local(queries, keys, values, out_grad, key_blocks, dilation):
    n = lax.axis_size("seq")
    tokens, width = queries.shape
    seq = tokens * n
    blocks = key_blocks.shape[1]
    row = jax.ShapeDtypeStruct((tokens, width), jnp.bfloat16)
    anywhere = pl.BlockSpec(memory_space=pl.ANY)
    work = [
        pltpu.VMEM((blocks, seq), jnp.float32),
        pltpu.VMEM((seq, 128), jnp.float32),
        pltpu.VMEM((HEAD_DIM, seq), jnp.bfloat16),
        pltpu.VMEM((HEAD_DIM, seq), jnp.bfloat16),
        pltpu.VMEM((seq, HEAD_DIM), jnp.float32),
        pltpu.VMEM((seq, HEAD_DIM), jnp.float32),
    ]
    if n == 8 and tokens == 128:
        heads = HEADS // 2
        half = seq // 2
        body = functools.partial(split_kernel, 8, 2)
        scratch = [
            pltpu.VMEM((heads, 4, half, HEAD_DIM), jnp.bfloat16),
            pltpu.VMEM((heads, 4, half, HEAD_DIM), jnp.bfloat16),
            pltpu.VMEM((heads, 2, half, HEAD_DIM), jnp.bfloat16),
            pltpu.VMEM((heads, 2, half, HEAD_DIM), jnp.bfloat16),
            pltpu.VMEM((heads, 4, tokens, HEAD_DIM), jnp.bfloat16),
            pltpu.VMEM((heads, 2, 2 * tokens, HEAD_DIM), jnp.float32),
            *work,
            *[pltpu.SemaphoreType.DMA((heads,))] * 7,
            pltpu.SemaphoreType.DMA((4,)),
            pltpu.SemaphoreType.DMA((1,)),
            pltpu.SemaphoreType.DMA((1,)),
        ]
    else:
        heads = HEADS // n
        body = functools.partial(kernel, n, heads)
        scratch = [
            pltpu.VMEM((heads, 4, seq, HEAD_DIM), jnp.bfloat16),
            pltpu.VMEM((heads, 4, seq, HEAD_DIM), jnp.bfloat16),
            *work,
            pltpu.SemaphoreType.DMA((heads,)),
            pltpu.SemaphoreType.DMA((heads,)),
            pltpu.SemaphoreType.DMA((heads,)),
            pltpu.SemaphoreType.DMA((4,)),
        ]
    results = pl.pallas_call(
        body,
        out_shape=(row,) * 4,
        in_specs=[anywhere] * 4
        + [pl.BlockSpec(memory_space=pltpu.VMEM), pl.BlockSpec(memory_space=pltpu.SMEM)],
        out_specs=(anywhere,) * 4,
        scratch_shapes=scratch,
        compiler_params=pltpu.CompilerParams(
            collective_id=0, has_side_effects=True, vmem_limit_bytes=56 * 1024 * 1024
        ),
    )(queries, keys, values, out_grad, jnp.transpose(key_blocks, (2, 1, 0)), dilation)
    return settle(results)


def solution(mesh):
    rows = P(("batch", "seq"), None)
    return jax.shard_map(
        local,
        mesh=mesh,
        in_specs=(rows, rows, rows, rows, P("batch", None, None), P("batch")),
        out_specs=(rows, rows, rows, rows),
        check_vma=False,
    )
```

```python
import functools
import math

import jax
import jax.numpy as jnp
from jax import lax
from jax.experimental import pallas as pl
from jax.experimental.pallas import tpu as pltpu
from jax.sharding import PartitionSpec as P

HEADS = 32
HEAD_DIM = 128
BLOCK = 64

very_low = -1e30
MESH = pl.DeviceIdType.MESH


def dot(a, b, dims):
    return lax.dot_general(a, b, (dims, ((), ())), preferred_element_type=jnp.float32)


LAST = ((1,), (1,))
PLAIN = ((1,), (0,))
FIRST = ((0,), (0,))


def build_masks(head, lists_ref, dilation_ref, row_codes, key_codes):
    slots, blocks, count = lists_ref.shape
    seq = row_codes.shape[1]
    spacing = dilation_ref[head].astype(jnp.float32)
    inverse = 1.0 / jnp.full((1, 128), spacing, jnp.float32)

    def residue(ids, inv):
        ids = ids.astype(jnp.float32)
        return ids - spacing * jnp.floor((ids + 0.5) * inv)

    mine = lax.broadcasted_iota(jnp.int32, (blocks, count), 1) == head
    key_ids = lax.broadcasted_iota(jnp.int32, (blocks, blocks), 1)
    member = jnp.zeros((blocks, blocks), jnp.float32)
    for slot in range(slots):
        listed = jnp.sum(jnp.where(mine, lists_ref[slot], 0), axis=1, keepdims=True)
        member = jnp.where(listed == key_ids, 1.0, member)
    spread = (
        lax.broadcasted_iota(jnp.int32, (blocks, seq), 1) // BLOCK
        == lax.broadcasted_iota(jnp.int32, (blocks, seq), 0)
    )
    listed = dot(member, spread.astype(jnp.float32), FIRST)
    query_ids = lax.broadcasted_iota(jnp.int32, (blocks, seq), 1)
    row_codes[...] = jnp.where(listed > 0.5, residue(query_ids, inverse[:, :1]), -1.0)
    key_codes[...] = residue(lax.broadcasted_iota(jnp.int32, (seq, 128), 0), inverse)


def attend_tile(
    start, chunks, diagonal_only, fresh, query, grad, key_at, value_at, attended, queries_grad, row_codes, key_codes, scratch
):
    keys_t, values_t, keys_sum, values_sum = scratch
    scale = 1.0 / math.sqrt(HEAD_DIM)
    tile = query.shape[0]
    rows = pl.ds(start, tile)
    chunk = 256
    query_ids = start + lax.broadcasted_iota(jnp.int32, (chunk, tile), 1)
    scores = []
    for c in range(chunks):
        span = slice(c * chunk, (c + 1) * chunk)
        raw = dot(key_at(c), query, LAST)
        codes = key_codes[span, :]
        codes = jnp.concatenate([codes] * (tile // 128), axis=1) if tile > 128 else codes
        first = c * chunk // BLOCK
        wanted = jnp.concatenate(
            [
                jnp.broadcast_to(row_codes[first + b : first + b + 1, rows], (BLOCK, tile))
                for b in range(chunk // BLOCK)
            ],
            axis=0,
        )
        seen = codes == wanted
        if not diagonal_only or c == chunks - 1:
            key_ids = c * chunk + lax.broadcasted_iota(jnp.int32, (chunk, tile), 0)
            seen = seen & (key_ids <= query_ids)
        scores.append(jnp.where(seen, raw, very_low / scale))
    top = functools.reduce(jnp.maximum, [jnp.max(s, axis=0, keepdims=True) for s in scores])
    yield
    expos, dweights = [], []
    for c in range(chunks):
        dweights.append(dot(value_at(c), grad, LAST))
        expos.append(jnp.exp2((scores[c] - top) * (scale * math.log2(math.e))))
    total = sum(jnp.sum(e, axis=0, keepdims=True) for e in expos)
    share = 1.0 / total
    grad_t = turned(grad).astype(jnp.float32)
    yield
    weights, out_t = [], None
    for c in range(chunks):
        span = slice(c * chunk, (c + 1) * chunk)
        weights.append(expos[c] * share)
        weights16 = weights[c].astype(jnp.bfloat16)
        part = dot(values_t[:, span], weights16, PLAIN)
        out_t = part if out_t is None else out_t + part
        part = dot(weights16, grad, PLAIN)
        values_sum[span, :] = part if fresh else values_sum[span, :] + part
    out16_t = out_t.astype(jnp.bfloat16)
    attended[...] = jnp.transpose(out16_t)
    delta = jnp.sum(grad_t * out16_t.astype(jnp.float32), axis=0, keepdims=True)
    yield
    query_t = None
    for c in range(chunks):
        span = slice(c * chunk, (c + 1) * chunk)
        dscores16 = (weights[c] * (dweights[c] - delta)).astype(jnp.bfloat16)
        part = dot(dscores16, query, PLAIN)
        keys_sum[span, :] = part if fresh else keys_sum[span, :] + part
        part = dot(keys_t[:, span], dscores16, PLAIN)
        query_t = part if query_t is None else query_t + part
    queries_grad[...] = jnp.transpose((query_t * scale).astype(jnp.bfloat16))
    yield


def turned(rows):
    return jnp.transpose(rows)


def attend_head(ins, outs, row_codes, key_codes, scratch):
    keys_t, values_t, keys_sum, values_sum = scratch
    queries, keys, values, grads = ins
    attended, queries_grad, keys_grad, values_grad = outs
    seq = keys.shape[0]
    keys_t[...] = turned(keys[...])
    values_t[...] = turned(values[...])
    keys_sum[...] = jnp.zeros_like(keys_sum)
    values_sum[...] = jnp.zeros_like(values_sum)

    def one(index, carry):
        start = pl.multiple_of(index * 128, 128)
        rows = pl.ds(start, 128)
        phases = attend_tile(
            start,
            seq // 256,
            False,
            False,
            queries[rows, :],
            grads[rows, :],
            lambda c: keys[c * 256 : (c + 1) * 256, :],
            lambda c: values[c * 256 : (c + 1) * 256, :],
            attended.at[rows, :],
            queries_grad.at[rows, :],
            row_codes,
            key_codes,
            scratch,
        )
        for _ in phases:
            pass
        return carry

    lax.fori_loop(0, seq // 128, one, 0)
    keys_grad[...] = (keys_sum[...] * (1.0 / math.sqrt(HEAD_DIM))).astype(jnp.bfloat16)
    values_grad[...] = values_sum[...].astype(jnp.bfloat16)


def attend_rows(key_chunks, query_tiles, held, made, row_codes, key_codes, scratch):
    keys_t, values_t, keys_sum, values_sum = scratch

    def rows_at(index, c):
        ref, first = key_chunks[c]
        return ref[index, first : first + 256, :]

    for c in range(len(key_chunks)):
        span = slice(c * 256, (c + 1) * 256)
        keys_t[:, span] = turned(rows_at(0, c))
        values_t[:, span] = turned(rows_at(1, c))
    tiles = []
    for number, (first, start) in enumerate(query_tiles):
        rows = slice(first, first + 256)
        phases = attend_tile(
            start,
            start // 256 + 1,
            True,
            number == 0,
            held[2, rows, :],
            held[3, rows, :],
            functools.partial(rows_at, 0),
            functools.partial(rows_at, 1),
            made.at[0, rows, :],
            made.at[1, rows, :],
            row_codes,
            key_codes,
            scratch,
        )
        tiles.append(phases)
    for _ in zip(*tiles):
        pass


def split_kernel(
    lag,
    lead,
    queries,
    keys,
    values,
    grads,
    lists_ref,
    dilation_ref,
    attended,
    queries_grad,
    keys_grad,
    values_grad,
    held,
    made,
    low_in,
    low_out,
    stage_out,
    sums,
    row_codes,
    key_codes,
    keys_t,
    values_t,
    keys_sum,
    values_sum,
    pair_recv,
    rest_recv,
    outer_recv,
    low_recv,
    part_recv,
    near_recv,
    stage_recv,
    out_recv,
    send,
    low_send,
):
    me = lax.axis_index("seq")
    tokens = queries.shape[0]
    heads = HEADS // 2
    pair = 2 * tokens
    half = 4 * tokens
    side = lax.rem(me, 2)
    plane = me // 2
    across = me + 1 - 2 * side
    sources = (keys, values, queries, grads)
    targets = (attended, queries_grad, keys_grad, values_grad)
    scale = 1.0 / math.sqrt(HEAD_DIM)
    scratch = (keys_t, values_t, keys_sum, values_sum)

    def at_plane(z):
        return 2 * z + side

    def columns(which, head):
        return pl.ds(pl.multiple_of((which * heads + head) * HEAD_DIM, HEAD_DIM), HEAD_DIM)

    def rows_of(device):
        return pl.ds(pl.multiple_of(lax.rem(device, 4) * tokens, tokens), tokens)

    def push(src, dst, send_sem, recv_sem, device):
        pltpu.make_async_remote_copy(
            src_ref=src,
            dst_ref=dst,
            send_sem=send_sem,
            recv_sem=recv_sem,
            device_id={"seq": device},
            device_id_type=MESH,
        ).start()

    def wait_for(ref, sem):
        pltpu.make_async_copy(ref, ref, sem).wait()

    def loop(count, body):
        def step(k, carry):
            body(k)
            return carry

        lax.fori_loop(0, count, step, 0)

    def enter(*others):
        barrier = pltpu.get_barrier_semaphore()
        for device in others:
            pl.semaphore_signal(barrier, inc=1, device_id={"seq": device}, device_id_type=MESH)
        pl.semaphore_wait(barrier, len(others))

    def arrival(index, k):
        return pair_recv.at[k] if index < 2 else rest_recv.at[k]

    def exchange(k, keep=True):
        for index, source in enumerate(sources):
            if keep:
                pltpu.make_async_copy(
                    source.at[:, columns(side, k)],
                    held.at[k, index, rows_of(me), :],
                    arrival(index, k),
                ).start()
            push(
                source.at[:, columns(1 - side, k)],
                held.at[k, index, rows_of(me), :],
                send.at[0],
                arrival(index, k),
                across,
            )

    def masks(k):
        build_masks(side * heads + k, lists_ref, dilation_ref, row_codes, key_codes)

    def give_near(index, k):
        target = targets[index]
        pltpu.make_async_copy(
            made.at[k, index, rows_of(me), :], target.at[:, columns(side, k)], out_recv.at[index]
        ).start()
        push(
            made.at[k, index, rows_of(across), :],
            target.at[:, columns(side, k)],
            send.at[0],
            out_recv.at[index],
            across,
        )

    def run_ahead(stages):
        for lead, body in stages:
            if lead > 0:
                loop(lead, body)

        def step(k):
            for lead, body in stages:
                if lead > 0:
                    pl.when(k + lead < heads)(functools.partial(body, k + lead))
                elif lead < 0:
                    pl.when(k + lead >= 0)(functools.partial(body, k + lead))
                else:
                    body(k)

        loop(heads, step)
        for lead, body in stages:
            if lead < 0:
                loop(-lead, lambda k, lead=lead, body=body: body(heads + lead + k))

    def add_up(k, rows, extra):
        for index in range(2):
            total = sums[k, index] + low_in[k, index, rows, :].astype(jnp.float32)
            if extra:
                total = total + low_out[k, index, rows, :].astype(jnp.float32)
            made[k, 2 + index, rows, :] = (total * (scale if index == 0 else 1.0)).astype(jnp.bfloat16)
            give_near(2 + index, k)

    def first_role():
        enter(across, at_plane(1), at_plane(2))
        rows = slice(0, pair)

        def forward(k):
            wait_for(held.at[k, pl.ds(0, 2), pl.ds(0, pair), :], pair_recv.at[k])
            block = held.at[k, pl.ds(0, 2), pl.ds(0, pair), :]
            push(block, low_in.at[k, :, pl.ds(0, pair), :], send.at[0], low_recv.at[k], at_plane(2))
            push(block, block, send.at[0], outer_recv.at[k], at_plane(1))

        def step(k):
            masks(k)
            wait_for(held.at[k, pl.ds(2, 2), pl.ds(0, pair), :], rest_recv.at[k])
            attend_rows(
                [(held.at[k], 0)], [(0, 0)], held.at[k], made.at[k], row_codes, key_codes, scratch
            )
            give_near(0, k)
            give_near(1, k)
            sums[k, 0] = keys_sum[rows, :]
            sums[k, 1] = values_sum[rows, :]

        def finish(k):
            wait_for(low_in.at[k, :, pl.ds(0, pair), :], part_recv.at[k])
            wait_for(low_out.at[k, :, pl.ds(0, pair), :], near_recv.at[k])
            add_up(k, rows, True)

        run_ahead([(2 * lead, exchange), (lead, forward), (0, step), (-lag, finish)])

    def second_role():
        enter(across, at_plane(0), at_plane(2))
        rows = slice(pair, half)

        def forward(k):
            block = held.at[k, pl.ds(0, 2), pl.ds(pair, pair), :]
            wait_for(block, pair_recv.at[k])
            push(block, low_in.at[k, :, pl.ds(pair, pair), :], send.at[0], low_recv.at[k], at_plane(2))

        def step(k):
            masks(k)
            wait_for(held.at[k, pl.ds(2, 2), pl.ds(pair, pair), :], rest_recv.at[k])
            wait_for(held.at[k, pl.ds(0, 2), pl.ds(0, pair), :], outer_recv.at[k])
            attend_rows(
                [(held.at[k], 0), (held.at[k], pair)],
                [(pair, pair)],
                held.at[k],
                made.at[k],
                row_codes,
                key_codes,
                scratch,
            )
            low_out[k, 0, :pair, :] = keys_sum[:pair, :].astype(jnp.bfloat16)
            low_out[k, 1, :pair, :] = values_sum[:pair, :].astype(jnp.bfloat16)
            block = low_out.at[k, :, pl.ds(0, pair), :]
            push(block, block, send.at[0], near_recv.at[k], at_plane(0))
            give_near(0, k)
            give_near(1, k)
            sums[k, 0] = keys_sum[rows, :]
            sums[k, 1] = values_sum[rows, :]

        def finish(k):
            wait_for(low_in.at[k, :, pl.ds(pair, pair), :], part_recv.at[k])
            add_up(k, rows, False)

        run_ahead([(2 * lead, exchange), (lead, forward), (0, step), (-lag, finish)])

    def third_role():
        enter(across, at_plane(0), at_plane(1), at_plane(3))

        def step(k):
            masks(k)
            wait_for(held.at[k, pl.ds(0, 2), pl.ds(0, pair), :], pair_recv.at[k])
            wait_for(held.at[k, pl.ds(2, 2), pl.ds(0, pair), :], rest_recv.at[k])
            wait_for(held.at[k, :, pl.ds(pair, pair), :], outer_recv.at[k])
            wait_for(low_in.at[k], low_recv.at[k])
            attend_rows(
                [(low_in.at[k], 0), (low_in.at[k], pair), (held.at[k], 0), (held.at[k], pair)],
                [(pair, half + pair), (0, half)],
                held.at[k],
                made.at[k],
                row_codes,
                key_codes,
                scratch,
            )
            low_out[k, 0] = keys_sum[:half, :].astype(jnp.bfloat16)
            low_out[k, 1] = values_sum[:half, :].astype(jnp.bfloat16)
            for z in range(2):
                block = pl.ds(z * pair, pair)
                push(
                    low_out.at[k, :, block, :],
                    low_in.at[k, :, block, :],
                    low_send.at[0],
                    part_recv.at[k],
                    at_plane(z),
                )
            made[k, 2] = (keys_sum[half:, :] * scale).astype(jnp.bfloat16)
            made[k, 3] = values_sum[half:, :].astype(jnp.bfloat16)
            along = at_plane(3)
            far = rows_of(along + 1 - 2 * side)
            push(made.at[k, :, far, :], stage_out.at[k], send.at[0], stage_recv.at[k], along)
            for index, target in enumerate(targets):
                push(
                    made.at[k, index, rows_of(along), :],
                    target.at[:, columns(side, k)],
                    send.at[0],
                    out_recv.at[index],
                    along,
                )
                give_near(index, k)

        run_ahead([(2 * lead, exchange), (0, step)])

    def fourth_role():
        enter(across, at_plane(2))

        def own(k):
            for index, source in enumerate(sources):
                push(
                    source.at[:, columns(side, k)],
                    held.at[k, index, rows_of(me), :],
                    send.at[0],
                    outer_recv.at[k],
                    at_plane(2),
                )

        def forward(k):
            for first, sem in ((0, pair_recv), (2, rest_recv)):
                block = held.at[k, pl.ds(first, 2), rows_of(across), :]
                wait_for(block, sem.at[k])
                push(block, block, send.at[0], outer_recv.at[k], at_plane(2))

        def finish(k):
            wait_for(stage_out.at[k], stage_recv.at[k])
            for index, target in enumerate(targets):
                push(
                    stage_out.at[k, index],
                    target.at[:, columns(side, k)],
                    send.at[0],
                    out_recv.at[index],
                    across,
                )

        exchange(0, False)
        own(0)
        loop(2 * lead - 1, lambda k: exchange(k + 1, False))

        def step(k):
            forward(k)
            pl.when(k + 1 < heads)(lambda: own(k + 1))
            pl.when(k + 2 * lead < heads)(lambda: exchange(k + 2 * lead, False))
            pl.when(k >= lag)(lambda: finish(k - lag))

        loop(heads, step)
        loop(lag, lambda k: finish(heads - lag + k))

    for z, role in enumerate((first_role, second_role, third_role, fourth_role)):
        pl.when(plane == z)(role)

    wait_for(held, send.at[0])
    pl.when(plane == 2)(lambda: wait_for(low_in, low_send.at[0]))
    for index, target in enumerate(targets):
        wait_for(target, out_recv.at[index])


def settle_kernel(pieces, *refs):
    sources, targets, slots, load, store = refs[:4], refs[4:8], refs[8], refs[9], refs[10]
    rows = sources[0].shape[0] // pieces
    loads, stores = [], []
    for index in range(4):
        for piece in range(pieces):
            span = pl.ds(piece * rows, rows)
            number = index * pieces + piece
            loads.append(
                pltpu.make_async_copy(sources[index].at[span, :], slots.at[index, span, :], load.at[number])
            )
            stores.append(
                pltpu.make_async_copy(slots.at[index, span, :], targets[index].at[span, :], store.at[number])
            )
    for copy in loads:
        copy.start()
    for arrived, copy in zip(loads, stores):
        arrived.wait()
        copy.start()
    for copy in stores:
        copy.wait()


def settle(arrays):
    rows, width = arrays[0].shape
    pieces = 4
    anywhere = pl.BlockSpec(memory_space=pl.ANY)
    return pl.pallas_call(
        functools.partial(settle_kernel, pieces),
        out_shape=(jax.ShapeDtypeStruct((rows, width), jnp.bfloat16),) * 4,
        in_specs=[anywhere] * 4,
        out_specs=(anywhere,) * 4,
        scratch_shapes=[
            pltpu.VMEM((4, rows, width), jnp.bfloat16),
            pltpu.SemaphoreType.DMA((4 * pieces,)),
            pltpu.SemaphoreType.DMA((4 * pieces,)),
        ],
        compiler_params=pltpu.CompilerParams(vmem_limit_bytes=56 * 1024 * 1024),
    )(*arrays)


def kernel(
    n,
    heads,
    queries,
    keys,
    values,
    grads,
    lists_ref,
    dilation_ref,
    attended,
    queries_grad,
    keys_grad,
    values_grad,
    held,
    made,
    row_codes,
    key_codes,
    keys_t,
    values_t,
    keys_sum,
    values_sum,
    in_send,
    in_recv,
    out_send,
    out_recv,
):
    me = lax.axis_index("seq")
    tokens = queries.shape[0]
    sources = (queries, keys, values, grads)
    targets = (attended, queries_grad, keys_grad, values_grad)
    my_rows = pl.ds(pl.multiple_of(me * tokens, tokens), tokens)

    def columns(owner, head):
        return pl.ds(pl.multiple_of((owner * heads + head) * HEAD_DIM, HEAD_DIM), HEAD_DIM)

    barrier = pltpu.get_barrier_semaphore()

    def greet(step, carry):
        pl.semaphore_signal(
            barrier, inc=1, device_id={"seq": lax.rem(me + step, n)}, device_id_type=MESH
        )
        return carry

    lax.fori_loop(1, n, greet, 0)
    pl.semaphore_wait(barrier, n - 1)

    def send_head(head, carry):
        def send_one(step, inner):
            other = lax.rem(me + step, n)
            for index, source in enumerate(sources):
                pltpu.make_async_remote_copy(
                    src_ref=source.at[:, columns(other, head)],
                    dst_ref=held.at[head, index, my_rows, :],
                    send_sem=in_send.at[head],
                    recv_sem=in_recv.at[head],
                    device_id={"seq": other},
                    device_id_type=MESH,
                ).start()
            return inner

        for index, source in enumerate(sources):
            pltpu.make_async_copy(
                source.at[:, columns(me, head)], held.at[head, index, my_rows, :], in_recv.at[head]
            ).start()
        lax.fori_loop(1, n, send_one, 0)
        return carry

    lax.fori_loop(0, heads, send_head, 0)

    def work_head(head, carry):
        build_masks(me * heads + head, lists_ref, dilation_ref, row_codes, key_codes)
        pltpu.make_async_copy(held.at[head], held.at[head], in_recv.at[head]).wait()
        attend_head(
            tuple(held.at[head, index] for index in range(4)),
            tuple(made.at[head, index] for index in range(4)),
            row_codes,
            key_codes,
            (keys_t, values_t, keys_sum, values_sum),
        )

        def send_one(step, inner):
            other = lax.rem(me + step, n)
            rows = pl.ds(pl.multiple_of(other * tokens, tokens), tokens)
            for index, target in enumerate(targets):
                pltpu.make_async_remote_copy(
                    src_ref=made.at[head, index, rows, :],
                    dst_ref=target.at[:, columns(me, head)],
                    send_sem=out_send.at[head],
                    recv_sem=out_recv.at[index],
                    device_id={"seq": other},
                    device_id_type=MESH,
                ).start()
            return inner

        for index, target in enumerate(targets):
            pltpu.make_async_copy(
                made.at[head, index, my_rows, :], target.at[:, columns(me, head)], out_recv.at[index]
            ).start()
        lax.fori_loop(1, n, send_one, 0)
        return carry

    lax.fori_loop(0, heads, work_head, 0)

    sent = (n - 1) * tokens

    def finish(head, carry):
        part = held.at[head, :, pl.ds(0, sent), :]
        pltpu.make_async_copy(part, part, in_send.at[head]).wait()
        part = made.at[head, :, pl.ds(0, sent), :]
        pltpu.make_async_copy(part, part, out_send.at[head]).wait()
        return carry

    lax.fori_loop(0, heads, finish, 0)
    for index, target in enumerate(targets):
        pltpu.make_async_copy(target, target, out_recv.at[index]).wait()


def local(queries, keys, values, out_grad, key_blocks, dilation):
    n = lax.axis_size("seq")
    tokens, width = queries.shape
    seq = tokens * n
    blocks = key_blocks.shape[1]
    row = jax.ShapeDtypeStruct((tokens, width), jnp.bfloat16)
    anywhere = pl.BlockSpec(memory_space=pl.ANY)
    work = [
        pltpu.VMEM((blocks, seq), jnp.float32),
        pltpu.VMEM((seq, 128), jnp.float32),
        pltpu.VMEM((HEAD_DIM, seq), jnp.bfloat16),
        pltpu.VMEM((HEAD_DIM, seq), jnp.bfloat16),
        pltpu.VMEM((seq, HEAD_DIM), jnp.float32),
        pltpu.VMEM((seq, HEAD_DIM), jnp.float32),
    ]
    if n == 8 and tokens == 128:
        heads = HEADS // 2
        half = seq // 2
        body = functools.partial(split_kernel, 8, 2)
        scratch = [
            pltpu.VMEM((heads, 4, half, HEAD_DIM), jnp.bfloat16),
            pltpu.VMEM((heads, 4, half, HEAD_DIM), jnp.bfloat16),
            pltpu.VMEM((heads, 2, half, HEAD_DIM), jnp.bfloat16),
            pltpu.VMEM((heads, 2, half, HEAD_DIM), jnp.bfloat16),
            pltpu.VMEM((heads, 4, tokens, HEAD_DIM), jnp.bfloat16),
            pltpu.VMEM((heads, 2, 2 * tokens, HEAD_DIM), jnp.float32),
            *work,
            *[pltpu.SemaphoreType.DMA((heads,))] * 7,
            pltpu.SemaphoreType.DMA((4,)),
            pltpu.SemaphoreType.DMA((1,)),
            pltpu.SemaphoreType.DMA((1,)),
        ]
    else:
        heads = HEADS // n
        body = functools.partial(kernel, n, heads)
        scratch = [
            pltpu.VMEM((heads, 4, seq, HEAD_DIM), jnp.bfloat16),
            pltpu.VMEM((heads, 4, seq, HEAD_DIM), jnp.bfloat16),
            *work,
            pltpu.SemaphoreType.DMA((heads,)),
            pltpu.SemaphoreType.DMA((heads,)),
            pltpu.SemaphoreType.DMA((heads,)),
            pltpu.SemaphoreType.DMA((4,)),
        ]
    results = pl.pallas_call(
        body,
        out_shape=(row,) * 4,
        in_specs=[anywhere] * 4
        + [pl.BlockSpec(memory_space=pltpu.VMEM), pl.BlockSpec(memory_space=pltpu.SMEM)],
        out_specs=(anywhere,) * 4,
        scratch_shapes=scratch,
        compiler_params=pltpu.CompilerParams(
            collective_id=0, has_side_effects=True, vmem_limit_bytes=56 * 1024 * 1024
        ),
    )(queries, keys, values, out_grad, jnp.transpose(key_blocks, (2, 1, 0)), dilation)
    return settle(results)


def solution(mesh):
    rows = P(("batch", "seq"), None)
    return jax.shard_map(
        local,
        mesh=mesh,
        in_specs=(rows, rows, rows, rows, P("batch", None, None), P("batch")),
        out_specs=(rows, rows, rows, rows),
        check_vma=False,
    )
```
